512 devices in a mesh: mem: 8 (over y_lo, x), grid: 64 (over z, y_hi, core).
Axes of the slice: x: 4, y: 8 (y_hi: 4, y_lo: 2; y = y_hi * 2 + y_lo), z: 8, core: 2. Of those that a mesh axis runs over, the one named last changes fastest.
Arguments:
- hidden: bfloat16 [8, 28672, 1024], P('mem', 'grid'), may hold values from -16 to 16
- predictions: bfloat16 [8, 100, 28672], P('mem', None, 'grid'), may hold values from -6 to 6
- target: bfloat16 [100, 28672], P(None, 'grid'), may hold values from -6 to 6
- area: float32 [28672], P('grid'), may hold values from 1 to 10
- var_weight: float32 [100], replicated, may hold values from 0.5 to 4
- interior: int32 [28672], P('grid'), may hold values 0 or 1
- sources: int32 [8, 28672], P(None, 'grid'), may hold values from 0 to 575
- edge_weight: float32 [8, 28672], P(None, 'grid'), may hold values from 0.05 to 0.25
- w_node: bfloat16 [1024, 1024], P('grid'), may hold values from -0.1875 to 0.1875
- w_dec: bfloat16 [1024, 100], replicated, may hold values from -0.1875 to 0.1875
Outputs:
- hidden_grad: bfloat16 [8, 28672, 1024], P('mem', 'grid')
- weight_grad: float32 [1024, 1024], P('grid')
- decoder_grad: float32 [1024, 100], replicated
The draws below stay inside these ranges and needn't reach their ends.
All inputs are finite; a program needn't handle non-finite values. No bound on the sum of `interior` on one device may be relied on, other than what follows from the above.
Results may differ from the reference program's by a relative error of at most 0.018.
Values may be sent and summed in bfloat16 or wider, within the bound.
No kernel may reach another device: no remote copies, remote signals or barrier semaphores. Data moves between devices by JAX's collectives and lax.ppermute only.
A program may use at most 64 MiB of HBM per device.

```python
import math
import jax
import jax.numpy as jnp
from jax import lax

D = 1024
V = 100
ND = 448
K = 64
KNB = 8
MEMBERS = 8
NODES = 28672
N_MEM = 8


def touch_ends(result, stream_key, least, largest):
    extent = result.shape
    place = [jax.random.randint(jax.random.fold_in(stream_key, axis), (), 0, extent[axis]) for axis in range(len(extent))]
    result = result.at[tuple(place)].set(least)
    longest = extent.index(max(extent))
    place[longest] = (place[longest] + 1) % extent[longest]
    return result.at[tuple(place)].set(largest)


def raised(entries, own_key, source, target, blocks, factor):
    owner, partner = [(jnp.arange(entries.shape[axis_at]) // (entries.shape[axis_at] // blocks)).reshape([-1 if axis == axis_at else 1 for axis in range(entries.ndim)]) for axis_at in (source, target)]
    chosen = jax.random.permutation(own_key, blocks)[partner]
    strong = (owner == chosen) | (owner == (partner + blocks // 2) % blocks)
    return jnp.where(strong, factor * entries, entries)


def block_scale(own_key, shape, pieces, smallest, largest):
    def one(axis_at, parts):
        draws = jax.random.uniform(jax.random.fold_in(jax.random.fold_in(own_key, 6), axis_at), (parts,), jnp.float32, smallest / len(pieces), largest / len(pieces))
        return jnp.repeat(jnp.exp(draws), shape[axis_at] // parts).reshape((-1,) + (1,) * (len(shape) - axis_at - 1))

    gain = one(*pieces[0])
    for cut in pieces[1:]:
        gain = gain * one(*cut)
    return gain


def normal_values(key, shape, scale, bound, shards=(), kind=jnp.bfloat16):
    result = scale * jax.random.normal(key, shape, jnp.float32)
    if shards:
        result = result * block_scale(key, shape, shards, -0.22, 0.18)
    return jnp.clip(result, -bound, bound).astype(kind)


def noise_with(key, extent, scale, reach, cuts, heavy, kind=jnp.bfloat16):
    result = scale * jax.random.normal(key, extent, jnp.float32)
    if cuts:
        result = result * block_scale(key, extent, cuts, -0.22, 0.18)
    return jnp.clip(raised(result, jax.random.fold_in(key, 3), *heavy), -reach, reach).astype(kind)


def setup_inputs(seed: int = 0) -> dict:
    keys = jax.random.split(jax.random.key(seed), 11)
    return {
        "hidden": noise_with(keys[0], (MEMBERS, NODES, D), 1.0, 16.0, ((0, 8), (1, 64)), (1, 2, 64, 4.0)),
        "predictions": normal_values(keys[1], (MEMBERS, V, NODES), 1.0, 6.0, ((0, 8), (2, 64))),
        "target": normal_values(keys[2], (V, NODES), 1.0, 6.0, ((1, 64),)),
        "area": jnp.clip(jnp.exp(math.log(10.0) - 2.3025851 * jax.random.uniform(keys[3], (NODES,), jnp.float32) ** block_scale(keys[3], (NODES,), ((0, 64),), -0.2, 0.2)), 1.0, 10.0),
        "var_weight": jnp.clip(jnp.exp(jax.random.uniform(keys[4], (V,), jnp.float32, math.log(0.5), math.log(4.0))), 0.5, 4.0),
        "interior": touch_ends((jax.random.randint(keys[5], (NODES,), 0, 8) < 7).astype(jnp.int32), jax.random.fold_in(keys[5], 1), 0, 1),
        "sources": touch_ends(jax.random.randint(keys[6], (KNB, NODES), 0, ND + 2 * K), jax.random.fold_in(keys[6], 1), 0, (ND + 2 * K) - 1).astype(jnp.int32),
        "edge_weight": jnp.clip(0.05 + 0.2 * jax.random.uniform(keys[7], (KNB, NODES), jnp.float32) ** block_scale(keys[7], (KNB, NODES), ((1, 64),), -0.2, 0.2), 0.05, 0.25),
        "w_node": normal_values(keys[8], (D, D), D ** -0.5, 0.1875, ((0, 64),)),
        "w_dec": normal_values(keys[9], (D, V), D ** -0.5, 0.1875),
    }


norm_eps = 1e-05
alpha_fair = 0.95
root_half = 1.0 / math.sqrt(2.0)
inv_root_two_pi = 1.0 / math.sqrt(2.0 * math.pi)

def reference(hidden, predictions, target, area, var_weight, interior, sources, edge_weight, w_node, w_dec):
    members = N_MEM
    coef_pair = (1.0 - (1.0 - alpha_fair) / members) / (members * (members - 1))
    node_ids = jnp.arange(NODES, dtype=jnp.int32)
    block_ids = node_ids // ND
    source_rows = (block_ids[None, :] * ND + sources - K).astype(jnp.int32)
    valid = (source_rows >= 0) & (source_rows < NODES)
    safe_rows = jnp.clip(source_rows, 0, NODES - 1).astype(jnp.int32)
    eff_weight = edge_weight * valid.astype(jnp.float32)
    pred_all = predictions.astype(jnp.float32)
    target_f = target.astype(jnp.float32)
    loss_weight = var_weight[:, None] * (area * interior.astype(jnp.float32))[None, :]

    def member_pass(pair_in):
        hid_m, pred_m = pair_in
        hid_f = hid_m.astype(jnp.float32)
        aggregate = jnp.zeros((NODES, D), jnp.float32)
        for slot in range(KNB):
            aggregate = aggregate + eff_weight[slot][:, None] * hid_f[safe_rows[slot]]
        layer_input = hid_f + aggregate
        centre = lax.optimization_barrier(jnp.mean(layer_input, axis=-1, keepdims=True))
        spread = lax.optimization_barrier(jnp.mean((layer_input - centre) ** 2, axis=-1, keepdims=True))
        inv_std = lax.rsqrt(spread + norm_eps)
        unit = (layer_input - centre) * inv_std
        normed = unit.astype(jnp.bfloat16)
        pre_act = jnp.dot(normed, w_node, preferred_element_type=jnp.float32)
        cdf_val = 0.5 * (1.0 + jax.scipy.special.erf(pre_act * root_half))
        layer_out = (layer_input + pre_act * cdf_val).astype(jnp.bfloat16)
        own_pred = pred_m.astype(jnp.float32)
        pair_sum = lax.optimization_barrier(jnp.sum(jnp.sign(own_pred[None] - pred_all), axis=0))
        pred_grad = (loss_weight * (jnp.sign(own_pred - target_f) / members - coef_pair * pair_sum)).astype(jnp.bfloat16)
        out_grad = lax.dot_general(pred_grad, w_dec, (((0,), (1,)), ((), ())), preferred_element_type=jnp.float32)
        pdf_val = jnp.exp(-0.5 * pre_act * pre_act) * inv_root_two_pi
        pre_grad = (out_grad * (cdf_val + pre_act * pdf_val)).astype(jnp.bfloat16)
        normed_grad = lax.dot_general(pre_grad, w_node, (((1,), (1,)), ((), ())), preferred_element_type=jnp.float32)
        mean_grad = lax.optimization_barrier(jnp.mean(normed_grad, axis=-1, keepdims=True))
        mean_cross = lax.optimization_barrier(jnp.mean(normed_grad * unit, axis=-1, keepdims=True))
        input_grad = out_grad + inv_std * (normed_grad - mean_grad - unit * mean_cross)
        total_grad = input_grad
        for slot in range(KNB):
            total_grad = total_grad.at[safe_rows[slot]].add(eff_weight[slot][:, None] * input_grad)
        weight_part = lax.dot_general(normed, pre_grad, (((0,), (0,)), ((), ())), preferred_element_type=jnp.float32)
        decoder_part = lax.dot_general(layer_out, pred_grad, (((0,), (1,)), ((), ())), preferred_element_type=jnp.float32)
        return (total_grad.astype(jnp.bfloat16), weight_part, decoder_part)
    hidden_grad, weight_parts, decoder_parts = lax.map(member_pass, (hidden, predictions))
    return (hidden_grad, lax.optimization_barrier(jnp.sum(weight_parts, axis=0)), lax.optimization_barrier(jnp.sum(decoder_parts, axis=0)))
```

```python
import math

import jax
import jax.numpy as jnp
from jax import lax
from jax.experimental import pallas as pl
from jax.experimental.pallas import tpu as pltpu
from jax.sharding import PartitionSpec as P

K = 64
KNB = 8
LANES = 128

norm_eps = 1e-05
alpha_fair = 0.95
root_half = 1.0 / math.sqrt(2.0)
inv_root_two_pi = 1.0 / math.sqrt(2.0 * math.pi)

f32 = jnp.float32
bf16 = jnp.bfloat16
VMEM = pl.BlockSpec(memory_space=pltpu.VMEM)
SMEM = pl.BlockSpec(memory_space=pltpu.SMEM)


def call(body, out, args, specs, scratch=(), flops=0, trans=0, mib=32, aliases=None):
    moved = sum(a.size * a.dtype.itemsize for a in args)
    moved += sum(math.prod(o.shape) * jnp.dtype(o.dtype).itemsize for o in out)
    return pl.pallas_call(
        body,
        out_shape=out,
        in_specs=specs,
        out_specs=[VMEM] * len(out),
        scratch_shapes=list(scratch),
        input_output_aliases=aliases or {},
        cost_estimate=pl.CostEstimate(flops=flops, bytes_accessed=moved, transcendentals=trans),
        compiler_params=pltpu.CompilerParams(vmem_limit_bytes=mib * 2**20),
    )(*args)


def shape(dims, dtype):
    return jax.ShapeDtypeStruct(dims, dtype)


def dot(a, b, ca=1, cb=0):
    return lax.dot_general(a, b, (((ca,), (cb,)), ((), ())), preferred_element_type=f32)


def edges_body(src_ref, ew_ref, at_ref):
    rows = at_ref.shape[0]
    nodes = at_ref.shape[1]
    step = 64
    for r in range(0, rows, step):
        j = lax.broadcasted_iota(jnp.int32, (step, nodes), 0) + r
        acc = jnp.zeros((step, nodes), f32)
        for s in range(KNB):
            acc += jnp.where(src_ref[s : s + 1, :] == j, ew_ref[s : s + 1, :], 0.0)
        at_ref[r : r + step, :] = acc.astype(bf16)


def norm_body(core_ref, own_ref, low_ref, high_ref, at_ref, normed_ref, rstd_ref, keep_ref, send_ref):
    core = core_ref[0]
    nodes, width = own_ref.shape
    half = width // 2
    agg = dot(at_ref[0:K, :], low_ref[...], 0, 0)
    agg += dot(at_ref[K : K + nodes, :], own_ref[...], 0, 0)
    agg += dot(at_ref[K + nodes :, :], high_ref[...], 0, 0)
    li = own_ref[...].astype(f32) + agg
    mean = jnp.mean(li, axis=-1, keepdims=True)
    dev = li - mean
    rstd = lax.rsqrt(jnp.mean(dev * dev, axis=-1, keepdims=True) + norm_eps)
    normed = (dev * rstd).astype(bf16)
    normed_ref[...] = normed
    rstd_ref[...] = jnp.broadcast_to(rstd, rstd_ref.shape)
    send_ref[:, 0:width] = normed
    lo = li[:, 0:half].astype(bf16)
    hi = li[:, half:].astype(bf16)

    @pl.when(core == 0)
    def _():
        keep_ref[...] = lo
        send_ref[:, width:] = hi

    @pl.when(core != 0)
    def _():
        keep_ref[...] = hi
        send_ref[:, width:] = lo


def fill_weight(wg_ref, w_ref):
    groups = w_ref.shape[0] // 32
    cols = w_ref.shape[1] // LANES
    for g in range(groups):
        for c in range(2):
            for x in range(cols):
                w_ref[g * 32 + c * 16 : g * 32 + c * 16 + 16, x * LANES : (x + 1) * LANES] = wg_ref[
                    c * cols + x, g * 16 : g * 16 + 16, :
                ]


def main_body(core_ref, wg_ref, no_ref, got_ref, keep_ref, po_ref, pp_ref, wd_ref, send_ref, pre_ref, w_ref, lo_ref):
    core = core_ref[0]
    nodes, width = no_ref.shape
    half = width // 2
    fill_weight(wg_ref, w_ref)
    wd = wd_ref[pl.ds(pl.multiple_of(core * half, half), half), :]
    step = nodes // 2
    for part in range(2):
        p_ref = (po_ref, pp_ref)[part]
        for r in range(0, nodes, step):
            n = no_ref[r : r + step, :] if part == 0 else got_ref[r : r + step, 0:width]
            li = keep_ref[r : r + step, :] if part == 0 else got_ref[r : r + step, width:]
            pre = dot(n, w_ref[...])
            og = dot(p_ref[r : r + step, :], wd, 1, 1)
            cdf = 0.5 * (1.0 + lax.erf(pre * root_half))
            pdf = jnp.exp(-0.5 * pre * pre) * inv_root_two_pi
            at = part * nodes + r
            lo_ref[at : at + step, :] = (li.astype(f32) + pre * cdf).astype(bf16)
            pre_ref[at : at + step, :] = (og * (cdf + pre * pdf)).astype(bf16)
    cols = half // LANES
    rows = 256
    groups = width // 32
    for q in range(0, width, rows):
        res = dot(no_ref[:, q : q + rows], pre_ref[0:nodes, :], 0, 0)
        res += dot(got_ref[:, q : q + rows], pre_ref[nodes:, :], 0, 0)
        res = res.astype(bf16)
        for g in range(rows // 32):
            for c in range(2):
                for x in range(cols):
                    at = (q // 32 + g) * 16
                    send_ref[c * cols + x, at : at + 16, :] = res[
                        g * 32 + c * 16 : g * 32 + c * 16 + 16, x * LANES : (x + 1) * LANES
                    ]
    dec = dot(lo_ref[0:nodes, :], po_ref[...], 0, 0) + dot(lo_ref[nodes:, :], pp_ref[...], 0, 0)
    dec = dec.astype(bf16)
    per = half // 8
    for m in range(8):
        send_ref[m, groups * 16 : groups * 16 + per, :] = dec[m * per : (m + 1) * per, :]
        send_ref[m, groups * 16 + per :, :] = jnp.zeros((send_ref.shape[1] - groups * 16 - per, LANES), bf16)


def sum_mem_body(got_ref, out_ref):
    groups = out_ref.shape[0]
    per = out_ref.shape[1] - 16
    total = got_ref[0, 0 : groups * 16 + per, :].astype(f32)
    for m in range(1, 8):
        total += got_ref[m, 0 : groups * 16 + per, :].astype(f32)
    total = total.astype(bf16)
    for g in range(groups):
        out_ref[g, 0:16, :] = total[g * 16 : g * 16 + 16, :]
        out_ref[g, 16:, :] = total[groups * 16 :, :]


def sum_grid_body(got_ref, out_ref):
    total = got_ref[0].astype(f32)
    for g in range(1, got_ref.shape[0]):
        total += got_ref[g].astype(f32)
    total = total.astype(bf16)
    for m in range(out_ref.shape[0]):
        out_ref[m] = total


def final_body(core_ref, got_ref, weight_ref, dec_ref):
    core = core_ref[0]
    per = got_ref.shape[1] - 16
    cols = weight_ref.shape[1] // 2 // LANES
    vars_ = dec_ref.shape[1]
    half = dec_ref.shape[0] // 2
    for c in range(2):
        for x in range(cols):
            lane = c * half + x * LANES
            weight_ref[:, lane : lane + LANES] = got_ref[(core * cols + x) * 2 + c, 0:16, :].astype(f32)
        for m in range(8):
            at = c * half + m * per
            dec_ref[at : at + per, :] = got_ref[m * 2 + c, 16:, 0:vars_].astype(f32)


def back_body(wg_ref, pre_ref, own_ref, send_ref, w_ref):
    nodes = own_ref.shape[0]
    fill_weight(wg_ref, w_ref)
    own_ref[...] = dot(pre_ref[0:nodes, :], w_ref[...], 1, 1)
    send_ref[...] = dot(pre_ref[nodes:, :], w_ref[...], 1, 1).astype(bf16)


def scatter_body(ng_ref, got_ref, no_ref, rstd_ref, po_ref, wd_ref, at_ref, mid_ref, edge_ref, prev_ref, next_ref):
    nodes = ng_ref.shape[0]
    ng = ng_ref[...] + got_ref[...].astype(f32)
    unit = no_ref[...].astype(f32)
    og = dot(po_ref[...], wd_ref[...], 1, 1)
    mean_g = jnp.mean(ng, axis=-1, keepdims=True)
    mean_c = jnp.mean(ng * unit, axis=-1, keepdims=True)
    ig = og + rstd_ref[:, 0:1] * (ng - mean_g - unit * mean_c)
    ib = ig.astype(bf16)
    prev_ref[...] = dot(at_ref[0:K, :], ib).astype(bf16)
    next_ref[...] = dot(at_ref[K + nodes :, :], ib).astype(bf16)
    core = ig + dot(at_ref[K : K + nodes, :], ib)
    mid_ref[...] = core.astype(bf16)
    edge_ref[0:K, :] = core[0:K, :]
    edge_ref[K:, :] = core[nodes - K :, :]


def join_body(mid_ref, edge_ref, prev_ref, next_ref, out_ref):
    nodes = mid_ref.shape[0]
    out_ref[0, 0:K, :] = (edge_ref[0:K, :] + prev_ref[...].astype(f32)).astype(bf16)
    out_ref[0, K : nodes - K, :] = mid_ref[K : nodes - K, :]
    out_ref[0, nodes - K :, :] = (edge_ref[K:, :] + next_ref[...].astype(f32)).astype(bf16)


def passed_along(shard, by):
    size = lax.axis_size(("pair", "core"))
    pairs = [(i, i + by) for i in range(size) if 0 <= i + by < size]
    return lax.ppermute(shard, ("pair", "core"), pairs)


def on_device(
    hidden, predictions, target, area, var_weight, interior, sources, edge_weight, w_node, w_dec
):
    members = lax.axis_size("mem")
    groups = lax.axis_size("pair")
    nodes, width = hidden.shape[1:]
    half = width // 2
    cols = half // LANES
    variables = w_dec.shape[1]
    coef_pair = (1.0 - (1.0 - alpha_fair) / members) / (members * (members - 1))
    core = lax.axis_index("core")
    member = lax.axis_index("mem")
    core_arg = core.astype(jnp.int32).reshape(1)
    own = hidden[0]
    def other_core(a):
        return lax.ppermute(a, "core", [(0, 1), (1, 0)])

    def over_grid(a):
        return lax.all_to_all(a, "pair", 0, 0, tiled=True)

    def over_mem(a):
        return lax.all_to_all(a, "mem", 0, 0, tiled=True)

    row_half, col_block = member // cols, member % cols
    tile_own = lax.dynamic_slice(w_node, (0, core * half + col_block * LANES), (16, LANES))
    tile_out = lax.dynamic_slice(w_node, (0, (1 - core) * half + col_block * LANES), (16, LANES))
    tile_got = other_core(tile_out)
    tile = jnp.where(core == row_half, tile_own, tile_got)
    shards = over_grid(jnp.broadcast_to(tile[None], (groups, 16, LANES)))
    weight = over_mem(jnp.broadcast_to(shards.reshape(1, groups * 16, LANES), (members, groups * 16, LANES)))

    low = passed_along(own[nodes - K :], 1)
    high = passed_along(own[:K], -1)
    every_pred = over_mem(jnp.broadcast_to(predictions, (members,) + predictions.shape[1:]))

    (at,) = call(
        edges_body, [shape((nodes + 2 * K, nodes), bf16)], (sources, edge_weight), [VMEM] * 2,
    )
    normed, rstd, keep, send = call(
        norm_body,
        [shape((nodes, width), bf16), shape((nodes, LANES), f32), shape((nodes, half), bf16),
         shape((nodes, width + half), bf16)],
        (core_arg, own, low, high, at),
        [SMEM] + [VMEM] * 4,
        flops=2 * nodes * (nodes + 2 * K) * width,
    )
    got = other_core(send)

    own_pred = predictions[0].astype(f32)
    loss_weight = var_weight[:, None] * (area * interior.astype(f32))[None, :]
    pair_sum = jnp.sum(jnp.sign(own_pred[None] - every_pred.astype(f32)), axis=0)
    grad_f = loss_weight * (jnp.sign(own_pred - target.astype(f32)) / members - coef_pair * pair_sum)
    pred_grad = jnp.pad(grad_f.astype(bf16), ((0, LANES - variables), (0, 0))).T
    pred_got = other_core(pred_grad)
    dec_pad = jnp.pad(w_dec, ((0, 0), (0, LANES - variables)))

    per = half // members
    sent_rows = groups * 16 + 2 * per
    parts, pre_grad = call(
        main_body,
        [shape((members, sent_rows, LANES), bf16), shape((2 * nodes, half), bf16)],
        (core_arg, weight, normed, got, keep, pred_grad, pred_got, dec_pad),
        [SMEM] + [VMEM] * 7,
        scratch=[pltpu.VMEM((width, half), bf16), pltpu.VMEM((2 * nodes, half), bf16)],
        flops=4 * 2 * nodes * width * half,
        trans=4 * nodes * half,
    )
    mem_parts = over_mem(parts)
    (grid_out,) = call(
        sum_mem_body, [shape((groups, 16 + per, LANES), bf16)], (mem_parts,), [VMEM],
    )
    grid_parts = over_grid(grid_out)
    (last_out,) = call(
        sum_grid_body, [shape((2 * members, 16 + per, LANES), bf16)], (grid_parts,), [VMEM],
    )
    last = lax.all_to_all(last_out, ("mem", "core"), 0, 0, tiled=True)
    weight_grad, decoder_grad = call(
        final_body,
        [shape((16, width), f32), shape((width, variables), f32)],
        (core_arg, last),
        [SMEM, VMEM],
    )

    ng_own, ng_send = call(
        back_body,
        [shape((nodes, width), f32), shape((nodes, width), bf16)],
        (weight, pre_grad),
        [VMEM] * 2,
        scratch=[pltpu.VMEM((width, half), bf16)],
        flops=4 * nodes * width * half,
    )
    ng_got = other_core(ng_send)
    mid, edge, to_prev, to_next = call(
        scatter_body,
        [shape((nodes, width), bf16), shape((2 * K, width), f32), shape((K, width), bf16),
         shape((K, width), bf16)],
        (ng_own, ng_got, normed, rstd, pred_grad, dec_pad, at),
        [VMEM] * 7,
        flops=2 * nodes * (nodes + 2 * K) * width,
    )
    from_next = passed_along(to_prev, -1)
    from_prev = passed_along(to_next, 1)
    (hidden_grad,) = call(
        join_body, [shape((1, nodes, width), bf16)], (mid, edge, from_prev, from_next), [VMEM] * 4,
    )
    return (hidden_grad, weight_grad, decoder_grad)


def solution(mesh):
    members, blocks = mesh.shape["mem"], mesh.shape["grid"]
    split = jax.sharding.Mesh(
        mesh.devices.reshape(members, blocks // 2, 2), ("mem", "pair", "core")
    )
    grid = ("pair", "core")
    placed = (
        P("mem", grid, None),
        P("mem", None, grid),
        P(None, grid),
        P(grid),
        P(),
        P(grid),
        P(None, grid),
        P(None, grid),
        P(grid, None),
        P(),
    )
    return jax.shard_map(
        on_device,
        mesh=split,
        in_specs=placed,
        out_specs=(P("mem", grid, None), P(grid, None), P()),
        check_vma=False,
    )
```

```python
import math

import jax
import jax.numpy as jnp
from jax import lax
from jax.experimental import pallas as pl
from jax.experimental.pallas import tpu as pltpu
from jax.sharding import PartitionSpec as P

K = 64
KNB = 8
LANES = 128
TILE = 16
MEMBERS = 8

norm_eps = 1e-05
alpha_fair = 0.95
root_half = 1.0 / math.sqrt(2.0)
inv_root_two_pi = 1.0 / math.sqrt(2.0 * math.pi)

f32 = jnp.float32
bf16 = jnp.bfloat16


def shape(dims, dtype):
    return jax.ShapeDtypeStruct(dims, dtype)


def dot(a, b, ca=1, cb=0):
    return lax.dot_general(a, b, (((ca,), (cb,)), ((), ())), preferred_element_type=f32)


class Copies:
    def __init__(self, sems):
        self.sems, self.used = sems, 0

    def start(self, src, dst):
        copy = pltpu.make_async_copy(src, dst, self.sems.at[self.used])
        self.used += 1
        copy.start()
        return copy


def after(x, *first):
    return lax.optimization_barrier((x,) + first)[0]


def sent(dims, dtype):
    return pltpu.HBM(dims, dtype)


def call(body, out, args, scratch=(), core=None, sems=0, hbm_args=(), flops=0, trans=0, mib=24):
    hbm_args = tuple(pltpu.with_memory_space_constraint(a, pltpu.HBM) for a in hbm_args)
    args = tuple(args) + hbm_args
    moved = sum(a.size * a.dtype.itemsize for a in args)
    moved += sum(math.prod(o.shape) * jnp.dtype(o.dtype).itemsize for o in out)
    first = [] if core is None else [core]

    def kernel(*refs):
        if sems:
            body(*refs[:-1], Copies(refs[-1]))
        else:
            body(*refs)

    vmem = pl.BlockSpec(memory_space=pltpu.VMEM)
    hbm = pl.BlockSpec(memory_space=pltpu.HBM)
    return pl.pallas_call(
        kernel,
        out_shape=out,
        in_specs=[pl.BlockSpec(memory_space=pltpu.SMEM)] * len(first) + [vmem] * (len(args) - len(hbm_args))
        + [hbm] * len(hbm_args),
        out_specs=[hbm if getattr(o, "memory_space", None) == pltpu.HBM else vmem for o in out],
        scratch_shapes=list(scratch) + ([pltpu.SemaphoreType.DMA((sems,))] if sems else []),
        cost_estimate=pl.CostEstimate(flops=flops, bytes_accessed=moved, transcendentals=trans),
        compiler_params=pltpu.CompilerParams(vmem_limit_bytes=mib * 2**20),
    )(*first, *args)


def widen_body(pred_ref, out_hbm, wide_ref, copies):
    variables, nodes = pred_ref.shape[1:]
    pad = jnp.zeros((wide_ref.shape[0] - variables, nodes), f32)
    wide_ref[...] = jnp.concatenate([pred_ref[0].astype(f32), pad], axis=0).astype(bf16)
    for c in [copies.start(wide_ref, out_hbm.at[m]) for m in range(MEMBERS)]:
        c.wait()


def tile_body(pick_ref, own_ref, got_ref, out_hbm, out_ref, copies):
    tile = jnp.where(pick_ref[0] == 1, own_ref[...].astype(f32), got_ref[...].astype(f32)).astype(bf16)
    out_ref[...] = jnp.broadcast_to(tile[None], out_ref.shape)
    copies.start(out_ref, out_hbm).wait()


def edges_body(src_ref, ew_ref, at_hbm, at_ref, copies):
    rows, nodes = at_ref.shape
    for r in range(0, rows, K):
        j = lax.broadcasted_iota(jnp.int32, (K, nodes), 0) + r
        acc = jnp.zeros((K, nodes), f32)
        for s in range(KNB):
            acc += jnp.where(src_ref[s : s + 1, :] == j, ew_ref[s : s + 1, :], 0.0)
        at_ref[r : r + K, :] = acc.astype(bf16)
    copies.start(at_ref, at_hbm).wait()


def norm_body(
    core_ref, own_ref, near_ref, far_ref, at_hbm, rstd_hbm, keep_hbm, send_hbm, at_ref, li_ref, normed_ref, rstd_ref, copies
):
    copies.start(at_hbm, at_ref).wait()
    core = core_ref[0]
    nodes, width = own_ref.shape
    half = width // 2
    near_at = pl.multiple_of((1 - core) * (K + nodes), K)
    far_at = pl.multiple_of(core * (K + nodes), K)
    agg = dot(at_ref[pl.ds(near_at, K), :], near_ref[...], 0, 0)
    agg += dot(at_ref[K : K + nodes, :], own_ref[...], 0, 0)
    agg += dot(at_ref[pl.ds(far_at, K), :], far_ref[...], 0, 0)
    li = own_ref[...].astype(f32) + agg
    li_ref[...] = li.astype(bf16)
    mine = pl.multiple_of(core * half, half)
    theirs = pl.multiple_of((1 - core) * half, half)
    stores = [
        copies.start(li_ref.at[:, pl.ds(theirs, half)], send_hbm.at[:, pl.ds(width, half)]),
        copies.start(li_ref.at[:, pl.ds(mine, half)], keep_hbm),
    ]
    mean = jnp.mean(li, axis=-1, keepdims=True)
    dev = li - mean
    rstd = lax.rsqrt(jnp.mean(dev * dev, axis=-1, keepdims=True) + norm_eps)
    normed_ref[...] = (dev * rstd).astype(bf16)
    stores.append(copies.start(normed_ref, send_hbm.at[:, pl.ds(0, width)]))
    rstd_ref[...] = jnp.broadcast_to(rstd, rstd_ref.shape)
    stores.append(copies.start(rstd_ref, rstd_hbm))
    for c in stores:
        c.wait()


def pred_body(all_ref, own_ref, target_ref, lw_ref, out_ref):
    members = all_ref.shape[0]
    variables = out_ref.shape[0]
    coef_pair = (1.0 - (1.0 - alpha_fair) / members) / (members * (members - 1))

    def sign(a):
        return jnp.where(a > 0.0, 1.0, jnp.where(a < 0.0, -1.0, 0.0))

    own = own_ref[0].astype(f32)
    pair_sum = jnp.zeros(own.shape, f32)
    for k in range(members):
        pair_sum += sign(own - all_ref[k].astype(f32)[0:variables])
    to_target = sign(own - target_ref[...].astype(f32))
    out_ref[...] = (lw_ref[...] * (to_target / members - coef_pair * pair_sum)).astype(bf16)


def share_body(got_ref, out_hbm, copies):
    for c in [copies.start(got_ref, out_hbm.at[m]) for m in range(out_hbm.shape[0])]:
        c.wait()


def fill_weight(wg_ref, w_ref):
    cols = w_ref.shape[1] // LANES
    for g in range(wg_ref.shape[1]):
        for c in range(2):
            for x in range(cols):
                at = (2 * g + c) * TILE
                w_ref[at : at + TILE, x * LANES : (x + 1) * LANES] = wg_ref[c * cols + x, g]


def main_body(
    core_ref, wg_ref, own_hbm, keep_hbm, po_hbm, wd_hbm, got_hbm, pp_hbm, send_hbm, pre_hbm, ng_hbm,
    no_ref, keep_ref, po_ref, wd_ref, got_ref, pp_ref, w_ref, lo_ref, pre_ref, parts_ref, ng_ref, copies,
):
    core = core_ref[0]
    nodes, width = no_ref.shape
    half = width // 2
    cols = half // LANES
    pairs = parts_ref.shape[1] - cols
    loads = [
        [copies.start(own_hbm.at[:, pl.ds(0, width)], no_ref), copies.start(keep_hbm, keep_ref),
         copies.start(po_hbm, po_ref), copies.start(wd_hbm, wd_ref)],
        [copies.start(got_hbm, got_ref), copies.start(pp_hbm, pp_ref)],
    ]
    fill_weight(wg_ref, w_ref)
    stores = []
    for part in range(2):
        p_ref = (po_ref, pp_ref)[part]
        for c in loads[part]:
            c.wait()
        wd = wd_ref[:, pl.ds(pl.multiple_of(core * half, half), half)]
        for r in range(0, nodes, 128):
            step = min(128, nodes - r)
            n = no_ref[r : r + step, :] if part == 0 else got_ref[r : r + step, 0:width]
            li = keep_ref[r : r + step, :] if part == 0 else got_ref[r : r + step, width:]
            pre = dot(n, w_ref[...])
            og = dot(p_ref[:, r : r + step], wd, 0, 0)
            cdf = 0.5 * (1.0 + lax.erf(pre * root_half))
            pdf = jnp.exp(-0.5 * pre * pre) * inv_root_two_pi
            at = part * nodes + r
            lo_ref[at : at + step, :] = (li.astype(f32) + pre * cdf).astype(bf16)
            pre_ref[at : at + step, :] = (og * (cdf + pre * pdf)).astype(bf16)
    stores.append(copies.start(pre_ref.at[pl.ds(0, nodes)], pre_hbm))
    ng_ref[...] = dot(pre_ref[nodes:, :], w_ref[...], 1, 1).astype(bf16)
    stores.append(copies.start(ng_ref, ng_hbm))
    dec = dot(po_ref[...], lo_ref[0:nodes, :]) + dot(pp_ref[...], lo_ref[nodes:, :])
    dec = jnp.concatenate([dec, jnp.zeros((MEMBERS * TILE - dec.shape[0], half), f32)], axis=0).astype(bf16)
    for m in range(MEMBERS):
        for x in range(cols):
            parts_ref[m, pairs + x] = dec[m * TILE : (m + 1) * TILE, x * LANES : (x + 1) * LANES]
    rows = 256
    for q in range(0, width, rows):
        res = dot(no_ref[:, q : q + rows], pre_ref[0:nodes, :], 0, 0)
        res += dot(got_ref[:, q : q + rows], pre_ref[nodes:, :], 0, 0)
        res = res.astype(bf16)
        first, count = q // (2 * TILE), rows // (2 * TILE)
        for g in range(count):
            for c in range(2):
                for x in range(cols):
                    at = (2 * g + c) * TILE
                    parts_ref[c * cols + x, first + g] = res[at : at + TILE, x * LANES : (x + 1) * LANES]
        last = q + rows == width
        tiles = pl.ds(first, count + (cols if last else 0))
        stores.append(copies.start(parts_ref.at[:, tiles], send_hbm.at[:, tiles]))
    for c in stores:
        c.wait()


def scatter_body(
    core_ref, wg_ref, got_ref, rstd_hbm, po_hbm, wd_hbm, pre_hbm, own_hbm, at_hbm, mid_hbm, edge_hbm, near_ref, far_ref,
    w_ref, rstd_ref, po_ref, wd_ref, pre_ref, no_ref, at_ref, ib_ref, mid_ref, edge_ref, copies,
):
    core = core_ref[0]
    nodes, width = no_ref.shape
    first = copies.start(pre_hbm, pre_ref)
    loads = [
        copies.start(po_hbm, po_ref),
        copies.start(wd_hbm, wd_ref),
        copies.start(own_hbm.at[:, pl.ds(0, width)], no_ref),
        copies.start(rstd_hbm, rstd_ref),
        copies.start(at_hbm, at_ref),
    ]
    fill_weight(wg_ref, w_ref)
    first.wait()
    ng = dot(pre_ref[...], w_ref[...], 1, 1) + got_ref[...].astype(f32)
    for c in loads:
        c.wait()
    unit = no_ref[...].astype(f32)
    og = dot(po_ref[...], wd_ref[...], 0, 0)
    mean_g = jnp.mean(ng, axis=-1, keepdims=True)
    mean_c = jnp.mean(ng * unit, axis=-1, keepdims=True)
    ig = og + rstd_ref[:, 0:1] * (ng - mean_g - unit * mean_c)
    ib_ref[...] = ig.astype(bf16)
    near_at = pl.multiple_of((1 - core) * (K + nodes), K)
    far_at = pl.multiple_of(core * (K + nodes), K)
    near_ref[...] = dot(at_ref[pl.ds(near_at, K), :], ib_ref[...]).astype(bf16)
    far_ref[...] = dot(at_ref[pl.ds(far_at, K), :], ib_ref[...]).astype(bf16)
    total = ig + dot(at_ref[K : K + nodes, :], ib_ref[...])
    mid_ref[...] = total.astype(bf16)
    edge_ref[0:K, :] = total[0:K, :]
    edge_ref[K:, :] = total[nodes - K :, :]
    for c in [copies.start(mid_ref, mid_hbm), copies.start(edge_ref, edge_hbm)]:
        c.wait()


def join_body(core_ref, near_ref, far_ref, mid_hbm, edge_hbm, out_hbm, mid_ref, edge_ref, copies):
    core = core_ref[0]
    nodes = mid_ref.shape[0]
    loads = [copies.start(mid_hbm, mid_ref), copies.start(edge_hbm, edge_ref)]
    for c in loads:
        c.wait()
    for ref, end in ((near_ref, 1 - core), (far_ref, core)):
        edge = edge_ref[pl.ds(pl.multiple_of(end * K, K), K), :] + ref[...].astype(f32)
        mid_ref[pl.ds(pl.multiple_of(end * (nodes - K), K), K), :] = edge.astype(bf16)
    copies.start(mid_ref, out_hbm.at[0]).wait()


def sum_mem_body(got_ref, out_hbm, out_ref, copies):
    pairs, tiles = out_ref.shape[:2]
    total = got_ref[0].astype(f32)
    for m in range(1, MEMBERS):
        total += got_ref[m].astype(f32)
    total = total.astype(bf16)
    out_ref[:, 0] = total[0:pairs]
    out_ref[:, 1:] = jnp.broadcast_to(total[pairs:][None], (pairs, tiles - 1, TILE, LANES))
    copies.start(out_ref, out_hbm).wait()


def sum_grid_body(got_ref, out_hbm, out_ref, copies):
    total = got_ref[0].astype(f32)
    for g in range(1, got_ref.shape[0]):
        total += got_ref[g].astype(f32)
    out_ref[...] = total.astype(bf16)
    for c in [copies.start(out_ref, out_hbm.at[m]) for m in range(out_hbm.shape[0])]:
        c.wait()


def final_body(core_ref, got_ref, weight_ref, dec_ref):
    core = core_ref[0]
    half = weight_ref.shape[1] // 2
    cols = half // LANES
    variables = dec_ref.shape[0]
    for c in range(2):
        for x in range(cols):
            lane = c * half + x * LANES
            weight_ref[:, lane : lane + LANES] = got_ref[(core * cols + x) * 2 + c, 0].astype(f32)
            for m in range(MEMBERS):
                rows = min(TILE, variables - m * TILE)
                if rows > 0:
                    tile = got_ref[m * 2 + c, 1 + x].astype(f32)
                    dec_ref[m * TILE : m * TILE + rows, lane : lane + LANES] = tile[0:rows, :]


def other_pair(a):
    size = lax.axis_size(("pair", "core"))
    pairs = [(i, i + (1 if i % 2 else -1)) for i in range(1, size - 1)]
    return lax.ppermute(a, ("pair", "core"), pairs)


def other_core(a):
    return lax.ppermute(a, "core", [(0, 1), (1, 0)])


def over_pairs(a):
    return lax.all_to_all(a, "pair", 0, 0, tiled=True)


def over_mem(a):
    return lax.all_to_all(a, "mem", 0, 0, tiled=True)


def on_device(
    hidden, predictions, target, area, var_weight, interior, sources, edge_weight, w_node, w_dec
):
    pairs = lax.axis_size("pair")
    nodes, width = hidden.shape[1:]
    half = width // 2
    cols = half // LANES
    variables = w_dec.shape[1]
    rows = -(-variables // TILE) * TILE
    core = lax.axis_index("core")
    member = lax.axis_index("mem")
    core_arg = core.astype(jnp.int32).reshape(1)
    own = hidden[0]
    vmem = pltpu.VMEM

    row_half, col_block = member // cols, member % cols
    tile_own = lax.dynamic_slice(w_node, (0, core * half + col_block * LANES), (TILE, LANES))
    tile_out = lax.dynamic_slice(w_node, (0, (1 - core) * half + col_block * LANES), (TILE, LANES))
    tile_got = other_core(tile_out)
    own_half = (core == row_half).astype(jnp.int32).reshape(1)
    (tiles,) = call(
        tile_body,
        [sent((pairs, TILE, LANES), bf16)],
        (tile_own, tile_got),
        [vmem((pairs, TILE, LANES), bf16)],
        core=own_half,
        sems=1,
    )

    (spread_pred,) = call(
        widen_body,
        [sent((MEMBERS, rows, nodes), bf16)],
        (predictions,),
        [vmem((rows, nodes), bf16)],
        sems=MEMBERS,
    )
    every_pred = over_mem(spread_pred)
    near = other_core(lax.dynamic_slice(own, ((1 - core) * (nodes - K), 0), (K, width)))
    far = other_pair(lax.dynamic_slice(own, (core * (nodes - K), 0), (K, width)))
    (at,) = call(
        edges_body, [sent((nodes + 2 * K, nodes), bf16)], (sources, edge_weight),
        [vmem((nodes + 2 * K, nodes), bf16)], sems=1,
    )
    shards = over_pairs(after(tiles, every_pred, far))
    rstd, keep, send = call(
        norm_body,
        [sent((nodes, LANES), f32), sent((nodes, half), bf16), sent((nodes, width + half), bf16)],
        (after(own, shards), near, far),
        [vmem((nodes + 2 * K, nodes), bf16), vmem((nodes, width), bf16), vmem((nodes, width), bf16),
         vmem((nodes, LANES), f32)],
        core=core_arg,
        hbm_args=(at,),
        sems=5,
        flops=2 * nodes * (nodes + 2 * K) * width,
    )
    got = other_core(send)
    loss_weight = var_weight[:, None] * (area * interior.astype(f32))[None, :]
    (pred_grad,) = call(
        pred_body,
        [shape((variables, nodes), bf16)],
        (every_pred, predictions, target, loss_weight),
    )
    pred_got = other_core(pred_grad)
    dec_t = w_dec.T

    (spread,) = call(
        share_body,
        [sent((MEMBERS, pairs, TILE, LANES), bf16)],
        (after(shards, pred_got, near, at),),
        sems=MEMBERS,
    )
    weight = over_mem(spread)

    weight_shape = vmem((width, half), bf16)
    part_shape = (MEMBERS, pairs + cols, TILE, LANES)
    parts, pre_grad, ng_send = call(
        main_body,
        [sent(part_shape, bf16), sent((nodes, half), bf16), sent((nodes, width), bf16)],
        (weight,),
        [vmem((nodes, width), bf16), vmem((nodes, half), bf16), vmem((variables, nodes), bf16),
         vmem((variables, width), bf16), vmem((nodes, width + half), bf16), vmem((variables, nodes), bf16), weight_shape, vmem((2 * nodes, half), bf16),
         vmem((2 * nodes, half), bf16), vmem(part_shape, bf16), vmem((nodes, width), bf16)],
        core=core_arg,
        hbm_args=(send, keep, pred_grad, dec_t, got, pred_got),
        sems=16,
        flops=5 * 2 * nodes * width * half,
        trans=4 * nodes * half,
    )
    mem_parts = over_mem(parts)

    ng_got = other_core(ng_send)
    mid, edge, to_near, to_far = call(
        scatter_body,
        [sent((nodes, width), bf16), sent((2 * K, width), f32), shape((K, width), bf16), shape((K, width), bf16)],
        (weight, ng_got),
        [weight_shape, vmem((nodes, LANES), f32), vmem((variables, nodes), bf16), vmem((variables, width), bf16),
         vmem((nodes, half), bf16), vmem((nodes, width), bf16), vmem((nodes + 2 * K, nodes), bf16),
         vmem((nodes, width), bf16), vmem((nodes, width), bf16), vmem((2 * K, width), f32)],
        core=core_arg,
        hbm_args=(rstd, pred_grad, dec_t, pre_grad, send, at),
        sems=8,
        flops=2 * nodes * (nodes + 2 * K) * width,
    )
    from_near = other_core(to_near)
    from_far = other_pair(to_far)
    (grid_out,) = call(
        sum_mem_body,
        [sent((pairs, 1 + cols, TILE, LANES), bf16)],
        (after(mem_parts, to_near),),
        [vmem((pairs, 1 + cols, TILE, LANES), bf16)],
        sems=1,
    )
    grid_parts = over_pairs(grid_out)
    (hidden_grad,) = call(
        join_body,
        [sent((1, nodes, width), bf16)],
        (from_near, from_far),
        [vmem((nodes, width), bf16), vmem((2 * K, width), f32)],
        core=core_arg,
        hbm_args=(mid, edge),
        sems=3,
    )
    (last_out,) = call(
        sum_grid_body,
        [sent((2 * MEMBERS, 1 + cols, TILE, LANES), bf16)],
        (after(grid_parts, from_near, from_far),),
        [vmem((1 + cols, TILE, LANES), bf16)],
        sems=2 * MEMBERS,
    )
    last = lax.all_to_all(last_out, ("mem", "core"), 0, 0, tiled=True)
    weight_grad, decoder_grad = call(
        final_body,
        [shape((TILE, width), f32), shape((variables, width), f32)],
        (last,),
        core=core_arg,
    )
    return (hidden_grad, weight_grad, decoder_grad.T)


def solution(mesh):
    members, blocks = mesh.shape["mem"], mesh.shape["grid"]
    split = jax.sharding.Mesh(
        mesh.devices.reshape(members, blocks // 2, 2), ("mem", "pair", "core")
    )
    grid = ("pair", "core")
    placed = (
        P("mem", grid, None),
        P("mem", None, grid),
        P(None, grid),
        P(grid),
        P(),
        P(grid),
        P(None, grid),
        P(None, grid),
        P(grid, None),
        P(),
    )
    return jax.shard_map(
        on_device,
        mesh=split,
        in_specs=placed,
        out_specs=(P("mem", grid, None), P(grid, None), P()),
        check_vma=False,
    )
```

```python
import math

import jax
import jax.numpy as jnp
from jax import lax
from jax.experimental import pallas as pl
from jax.experimental.pallas import tpu as pltpu
from jax.sharding import PartitionSpec as P

K = 64
KNB = 8
LANES = 128
TILE = 16
DEC_TILES = 4
MEMBERS = 8
GRID = ("z", "y", "core")
PAIR = ("z", "y")

norm_eps = 1e-05
alpha_fair = 0.95
root_half = 1.0 / math.sqrt(2.0)
inv_root_two_pi = 1.0 / math.sqrt(2.0 * math.pi)

f32 = jnp.float32
bf16 = jnp.bfloat16


def shape(dims, dtype):
    return jax.ShapeDtypeStruct(dims, dtype)


def dot(a, b, ca=1, cb=0):
    return lax.dot_general(a, b, (((ca,), (cb,)), ((), ())), preferred_element_type=f32)


class Copies:
    def __init__(self, sems):
        self.sems, self.used = sems, 0

    def start(self, src, dst):
        copy = pltpu.make_async_copy(src, dst, self.sems.at[self.used])
        self.used += 1
        copy.start()
        return copy


def after(x, *first):
    return lax.optimization_barrier((x,) + first)[0]


def sent(dims, dtype):
    return pltpu.HBM(dims, dtype)


def call(body, out, args, scratch=(), core=None, sems=0, hbm_args=(), flops=0, trans=0, mib=24):
    hbm_args = tuple(pltpu.with_memory_space_constraint(a, pltpu.HBM) for a in hbm_args)
    args = tuple(args) + hbm_args
    moved = sum(a.size * a.dtype.itemsize for a in args)
    moved += sum(math.prod(o.shape) * jnp.dtype(o.dtype).itemsize for o in out)
    first = [] if core is None else [core]

    def kernel(*refs):
        if sems:
            body(*refs[:-1], Copies(refs[-1]))
        else:
            body(*refs)

    vmem = pl.BlockSpec(memory_space=pltpu.VMEM)
    hbm = pl.BlockSpec(memory_space=pltpu.HBM)
    return pl.pallas_call(
        kernel,
        out_shape=out,
        in_specs=[pl.BlockSpec(memory_space=pltpu.SMEM)] * len(first) + [vmem] * (len(args) - len(hbm_args))
        + [hbm] * len(hbm_args),
        out_specs=[hbm if getattr(o, "memory_space", None) == pltpu.HBM else vmem for o in out],
        scratch_shapes=list(scratch) + ([pltpu.SemaphoreType.DMA((sems,))] if sems else []),
        cost_estimate=pl.CostEstimate(flops=flops, bytes_accessed=moved, transcendentals=trans),
        compiler_params=pltpu.CompilerParams(vmem_limit_bytes=mib * 2**20),
    )(*first, *args)


def widen_body(pred_ref, out_hbm, wide_ref, copies):
    variables, nodes = pred_ref.shape[1:]
    pad = jnp.zeros((wide_ref.shape[0] - variables, nodes), f32)
    wide_ref[...] = jnp.concatenate([pred_ref[0].astype(f32), pad], axis=0).astype(bf16)
    for c in [copies.start(wide_ref, out_hbm.at[m]) for m in range(MEMBERS)]:
        c.wait()


def tile_body(pick_ref, own_ref, got_ref, out_hbm, out_ref, copies):
    tile = jnp.where(pick_ref[0] == 1, own_ref[...].astype(f32), got_ref[...].astype(f32)).astype(bf16)
    out_ref[...] = jnp.broadcast_to(tile[None], out_ref.shape)
    copies.start(out_ref, out_hbm).wait()


def edges_body(src_ref, ew_ref, at_hbm, at_ref, copies):
    rows, nodes = at_ref.shape
    for r in range(0, rows, K):
        j = lax.broadcasted_iota(jnp.int32, (K, nodes), 0) + r
        acc = jnp.zeros((K, nodes), f32)
        for s in range(KNB):
            acc += jnp.where(src_ref[s : s + 1, :] == j, ew_ref[s : s + 1, :], 0.0)
        at_ref[r : r + K, :] = acc.astype(bf16)
    copies.start(at_ref, at_hbm).wait()


def norm_body(
    core_ref, own_ref, near_ref, far_ref, at_hbm, rstd_hbm, keep_hbm, send_hbm, at_ref, li_ref, normed_ref, rstd_ref, copies
):
    copies.start(at_hbm, at_ref).wait()
    core = core_ref[0]
    nodes, width = own_ref.shape
    half = width // 2
    near_at = pl.multiple_of((1 - core) * (K + nodes), K)
    far_at = pl.multiple_of(core * (K + nodes), K)
    agg = dot(at_ref[pl.ds(near_at, K), :], near_ref[...], 0, 0)
    agg += dot(at_ref[K : K + nodes, :], own_ref[...], 0, 0)
    agg += dot(at_ref[pl.ds(far_at, K), :], far_ref[...], 0, 0)
    li = own_ref[...].astype(f32) + agg
    li_ref[...] = li.astype(bf16)
    mine = pl.multiple_of(core * half, half)
    theirs = pl.multiple_of((1 - core) * half, half)
    stores = [
        copies.start(li_ref.at[:, pl.ds(theirs, half)], send_hbm.at[:, pl.ds(width, half)]),
        copies.start(li_ref.at[:, pl.ds(mine, half)], keep_hbm),
    ]
    mean = jnp.mean(li, axis=-1, keepdims=True)
    dev = li - mean
    rstd = lax.rsqrt(jnp.mean(dev * dev, axis=-1, keepdims=True) + norm_eps)
    normed_ref[...] = (dev * rstd).astype(bf16)
    stores.append(copies.start(normed_ref, send_hbm.at[:, pl.ds(0, width)]))
    rstd_ref[...] = jnp.broadcast_to(rstd, rstd_ref.shape)
    stores.append(copies.start(rstd_ref, rstd_hbm))
    for c in stores:
        c.wait()


def pred_body(all_ref, own_ref, target_ref, lw_ref, out_ref):
    members = all_ref.shape[0]
    variables = out_ref.shape[0]
    coef_pair = (1.0 - (1.0 - alpha_fair) / members) / (members * (members - 1))

    def sign(a):
        return jnp.where(a > 0.0, 1.0, jnp.where(a < 0.0, -1.0, 0.0))

    own = own_ref[0].astype(f32)
    pair_sum = jnp.zeros(own.shape, f32)
    for k in range(members):
        pair_sum += sign(own - all_ref[k].astype(f32)[0:variables])
    to_target = sign(own - target_ref[...].astype(f32))
    out_ref[...] = (lw_ref[...] * (to_target / members - coef_pair * pair_sum)).astype(bf16)


def share_body(got_ref, out_hbm, copies):
    for c in [copies.start(got_ref, out_hbm.at[m]) for m in range(out_hbm.shape[0])]:
        c.wait()


def fill_weight(wg_ref, w_ref):
    cols = w_ref.shape[1] // LANES
    for g in range(wg_ref.shape[1]):
        for c in range(2):
            for x in range(cols):
                at = (2 * g + c) * TILE
                w_ref[at : at + TILE, x * LANES : (x + 1) * LANES] = wg_ref[c * cols + x, g]


def main_body(
    core_ref, wg_ref, own_hbm, keep_hbm, po_hbm, wd_hbm, got_hbm, pp_hbm, send_hbm, pre_hbm, ng_hbm,
    no_ref, keep_ref, po_ref, wd_ref, got_ref, pp_ref, w_ref, lo_ref, pre_ref, parts_ref, ng_ref, copies,
):
    core = core_ref[0]
    nodes, width = no_ref.shape
    half = width // 2
    cols = half // LANES
    pairs = parts_ref.shape[1] - cols
    loads = [
        [copies.start(own_hbm.at[:, pl.ds(0, width)], no_ref), copies.start(keep_hbm, keep_ref),
         copies.start(po_hbm, po_ref), copies.start(wd_hbm, wd_ref)],
        [copies.start(got_hbm, got_ref), copies.start(pp_hbm, pp_ref)],
    ]
    fill_weight(wg_ref, w_ref)
    stores = []
    for part in range(2):
        p_ref = (po_ref, pp_ref)[part]
        for c in loads[part]:
            c.wait()
        wd = wd_ref[:, pl.ds(pl.multiple_of(core * half, half), half)]
        for r in range(0, nodes, 128):
            step = min(128, nodes - r)
            n = no_ref[r : r + step, :] if part == 0 else got_ref[r : r + step, 0:width]
            li = keep_ref[r : r + step, :] if part == 0 else got_ref[r : r + step, width:]
            pre = dot(n, w_ref[...])
            og = dot(p_ref[:, r : r + step], wd, 0, 0)
            cdf = 0.5 * (1.0 + lax.erf(pre * root_half))
            pdf = jnp.exp(-0.5 * pre * pre) * inv_root_two_pi
            at = part * nodes + r
            lo_ref[at : at + step, :] = (li.astype(f32) + pre * cdf).astype(bf16)
            pre_ref[at : at + step, :] = (og * (cdf + pre * pdf)).astype(bf16)
    stores.append(copies.start(pre_ref.at[pl.ds(0, nodes)], pre_hbm))
    ng_ref[...] = dot(pre_ref[nodes:, :], w_ref[...], 1, 1).astype(bf16)
    stores.append(copies.start(ng_ref, ng_hbm))
    dec = dot(po_ref[...], lo_ref[0:nodes, :]) + dot(pp_ref[...], lo_ref[nodes:, :])
    dec = jnp.concatenate([dec, jnp.zeros((MEMBERS * TILE - dec.shape[0], half), f32)], axis=0).astype(bf16)
    for m in range(MEMBERS):
        for x in range(cols):
            parts_ref[m, pairs + x] = dec[m * TILE : (m + 1) * TILE, x * LANES : (x + 1) * LANES]
    rows = 256
    for q in range(0, width, rows):
        res = dot(no_ref[:, q : q + rows], pre_ref[0:nodes, :], 0, 0)
        res += dot(got_ref[:, q : q + rows], pre_ref[nodes:, :], 0, 0)
        res = res.astype(bf16)
        first, count = q // (2 * TILE), rows // (2 * TILE)
        for g in range(count):
            for c in range(2):
                for x in range(cols):
                    at = (2 * g + c) * TILE
                    parts_ref[c * cols + x, first + g] = res[at : at + TILE, x * LANES : (x + 1) * LANES]
        last = q + rows == width
        tiles = pl.ds(first, count + (cols if last else 0))
        stores.append(copies.start(parts_ref.at[:, tiles], send_hbm.at[:, tiles]))
    for c in stores:
        c.wait()


def scatter_body(
    core_ref, wg_ref, got_ref, rstd_hbm, po_hbm, wd_hbm, pre_hbm, own_hbm, at_hbm, mid_hbm, edge_hbm, near_ref, far_ref,
    w_ref, rstd_ref, po_ref, wd_ref, pre_ref, no_ref, at_ref, ib_ref, mid_ref, edge_ref, copies,
):
    core = core_ref[0]
    nodes, width = no_ref.shape
    first = copies.start(pre_hbm, pre_ref)
    loads = [
        copies.start(po_hbm, po_ref),
        copies.start(wd_hbm, wd_ref),
        copies.start(own_hbm.at[:, pl.ds(0, width)], no_ref),
        copies.start(rstd_hbm, rstd_ref),
        copies.start(at_hbm, at_ref),
    ]
    fill_weight(wg_ref, w_ref)
    first.wait()
    ng = dot(pre_ref[...], w_ref[...], 1, 1) + got_ref[...].astype(f32)
    for c in loads:
        c.wait()
    unit = no_ref[...].astype(f32)
    og = dot(po_ref[...], wd_ref[...], 0, 0)
    mean_g = jnp.mean(ng, axis=-1, keepdims=True)
    mean_c = jnp.mean(ng * unit, axis=-1, keepdims=True)
    ig = og + rstd_ref[:, 0:1] * (ng - mean_g - unit * mean_c)
    ib_ref[...] = ig.astype(bf16)
    near_at = pl.multiple_of((1 - core) * (K + nodes), K)
    far_at = pl.multiple_of(core * (K + nodes), K)
    near_ref[...] = dot(at_ref[pl.ds(near_at, K), :], ib_ref[...]).astype(bf16)
    far_ref[...] = dot(at_ref[pl.ds(far_at, K), :], ib_ref[...]).astype(bf16)
    total = ig + dot(at_ref[K : K + nodes, :], ib_ref[...])
    mid_ref[...] = total.astype(bf16)
    edge_ref[0:K, :] = total[0:K, :]
    edge_ref[K:, :] = total[nodes - K :, :]
    for c in [copies.start(mid_ref, mid_hbm), copies.start(edge_ref, edge_hbm)]:
        c.wait()


def join_body(core_ref, near_ref, far_ref, mid_hbm, edge_hbm, out_hbm, mid_ref, edge_ref, copies):
    core = core_ref[0]
    nodes = mid_ref.shape[0]
    loads = [copies.start(mid_hbm, mid_ref), copies.start(edge_hbm, edge_ref)]
    for c in loads:
        c.wait()
    for ref, end in ((near_ref, 1 - core), (far_ref, core)):
        edge = edge_ref[pl.ds(pl.multiple_of(end * K, K), K), :] + ref[...].astype(f32)
        mid_ref[pl.ds(pl.multiple_of(end * (nodes - K), K), K), :] = edge.astype(bf16)
    copies.start(mid_ref, out_hbm.at[0]).wait()


def total_of(got_ref):
    total = got_ref[0].astype(f32)
    for i in range(1, got_ref.shape[0]):
        total += got_ref[i].astype(f32)
    return total.astype(bf16)


def sum_body(got_ref, out_hbm, out_ref, copies):
    total = total_of(got_ref)
    parts, tiles = out_ref.shape[:2]
    dec = DEC_TILES
    weights = got_ref.shape[1] - dec
    each = weights // parts
    out_ref[:, 0:each] = total[0:weights].reshape(parts, each, TILE, LANES)
    out_ref[:, each:] = jnp.broadcast_to(total[weights:][None], (parts, dec, TILE, LANES))
    copies.start(out_ref, out_hbm).wait()


def sum_last_body(got_ref, out_hbm, out_ref, copies):
    out_ref[...] = total_of(got_ref)
    for c in [copies.start(out_ref, out_hbm.at[m]) for m in range(out_hbm.shape[0])]:
        c.wait()


def final_body(core_ref, got_ref, weight_ref, dec_ref):
    core = core_ref[0]
    half = weight_ref.shape[1] // 2
    cols = half // LANES
    variables = dec_ref.shape[0]
    for c in range(2):
        for x in range(cols):
            lane = c * half + x * LANES
            weight_ref[:, lane : lane + LANES] = got_ref[(core * cols + x) * 2 + c, 0].astype(f32)
            for m in range(MEMBERS):
                rows = min(TILE, variables - m * TILE)
                if rows > 0:
                    tile = got_ref[m * 2 + c, 1 + x].astype(f32)
                    dec_ref[m * TILE : m * TILE + rows, lane : lane + LANES] = tile[0:rows, :]


def other_pair(a):
    size = lax.axis_size(GRID)
    pairs = [(i, i + (1 if i % 2 else -1)) for i in range(1, size - 1)]
    return lax.ppermute(a, GRID, pairs)


def other_core(a):
    return lax.ppermute(a, "core", [(0, 1), (1, 0)])


def over_pairs(a):
    return lax.all_to_all(a, PAIR, 0, 0, tiled=True)


def over_mem(a):
    return lax.all_to_all(a, "mem", 0, 0, tiled=True)


def on_device(
    hidden, predictions, target, area, var_weight, interior, sources, edge_weight, w_node, w_dec
):
    pairs = lax.axis_size(PAIR)
    nodes, width = hidden.shape[1:]
    half = width // 2
    cols = half // LANES
    variables = w_dec.shape[1]
    rows = -(-variables // TILE) * TILE
    core = lax.axis_index("core")
    member = lax.axis_index("mem")
    core_arg = core.astype(jnp.int32).reshape(1)
    own = hidden[0]
    vmem = pltpu.VMEM

    row_half, col_block = member // cols, member % cols
    tile_own = lax.dynamic_slice(w_node, (0, core * half + col_block * LANES), (TILE, LANES))
    tile_out = lax.dynamic_slice(w_node, (0, (1 - core) * half + col_block * LANES), (TILE, LANES))
    tile_got = other_core(tile_out)
    own_half = (core == row_half).astype(jnp.int32).reshape(1)
    (tiles,) = call(
        tile_body,
        [sent((pairs, TILE, LANES), bf16)],
        (tile_own, tile_got),
        [vmem((pairs, TILE, LANES), bf16)],
        core=own_half,
        sems=1,
    )

    (spread_pred,) = call(
        widen_body,
        [sent((MEMBERS, rows, nodes), bf16)],
        (predictions,),
        [vmem((rows, nodes), bf16)],
        sems=MEMBERS,
    )
    every_pred = over_mem(spread_pred)
    near = other_core(lax.dynamic_slice(own, ((1 - core) * (nodes - K), 0), (K, width)))
    far = other_pair(lax.dynamic_slice(own, (core * (nodes - K), 0), (K, width)))
    (at,) = call(
        edges_body, [sent((nodes + 2 * K, nodes), bf16)], (sources, edge_weight),
        [vmem((nodes + 2 * K, nodes), bf16)], sems=1,
    )
    shards = over_pairs(after(tiles, every_pred))
    rstd, keep, send = call(
        norm_body,
        [sent((nodes, LANES), f32), sent((nodes, half), bf16), sent((nodes, width + half), bf16)],
        (after(own, shards), near, far),
        [vmem((nodes + 2 * K, nodes), bf16), vmem((nodes, width), bf16), vmem((nodes, width), bf16),
         vmem((nodes, LANES), f32)],
        core=core_arg,
        hbm_args=(at,),
        sems=5,
        flops=2 * nodes * (nodes + 2 * K) * width,
    )
    got = other_core(send)
    loss_weight = var_weight[:, None] * (area * interior.astype(f32))[None, :]
    (pred_grad,) = call(
        pred_body,
        [shape((variables, nodes), bf16)],
        (every_pred, predictions, target, loss_weight),
    )
    pred_got = other_core(pred_grad)
    dec_t = w_dec.T

    (spread,) = call(
        share_body,
        [sent((MEMBERS, pairs, TILE, LANES), bf16)],
        (after(shards, pred_got, near, far, at),),
        sems=MEMBERS,
    )
    weight = over_mem(spread)

    weight_shape = vmem((width, half), bf16)
    part_shape = (MEMBERS, pairs + cols, TILE, LANES)
    parts, pre_grad, ng_send = call(
        main_body,
        [sent(part_shape, bf16), sent((nodes, half), bf16), sent((nodes, width), bf16)],
        (weight,),
        [vmem((nodes, width), bf16), vmem((nodes, half), bf16), vmem((variables, nodes), bf16),
         vmem((variables, width), bf16), vmem((nodes, width + half), bf16), vmem((variables, nodes), bf16), weight_shape, vmem((2 * nodes, half), bf16),
         vmem((2 * nodes, half), bf16), vmem(part_shape, bf16), vmem((nodes, width), bf16)],
        core=core_arg,
        hbm_args=(send, keep, pred_grad, dec_t, got, pred_got),
        sems=16,
        flops=5 * 2 * nodes * width * half,
        trans=4 * nodes * half,
    )
    mem_parts = over_mem(parts)

    ng_got = other_core(ng_send)
    mid, edge, to_near, to_far = call(
        scatter_body,
        [sent((nodes, width), bf16), sent((2 * K, width), f32), shape((K, width), bf16), shape((K, width), bf16)],
        (weight, ng_got),
        [weight_shape, vmem((nodes, LANES), f32), vmem((variables, nodes), bf16), vmem((variables, width), bf16),
         vmem((nodes, half), bf16), vmem((nodes, width), bf16), vmem((nodes + 2 * K, nodes), bf16),
         vmem((nodes, width), bf16), vmem((nodes, width), bf16), vmem((2 * K, width), f32)],
        core=core_arg,
        hbm_args=(rstd, pred_grad, dec_t, pre_grad, send, at),
        sems=8,
        flops=2 * nodes * (nodes + 2 * K) * width,
    )
    from_near = other_core(to_near)
    from_far = other_pair(to_far)
    n_z, n_y = lax.axis_size("z"), lax.axis_size("y")
    (z_out,) = call(
        sum_body,
        [sent((n_z, n_y + cols, TILE, LANES), bf16)],
        (after(mem_parts, to_near),),
        [vmem((n_z, n_y + cols, TILE, LANES), bf16)],
        sems=1,
    )
    z_parts = lax.all_to_all(z_out, "z", 0, 0, tiled=True)
    (y_out,) = call(
        sum_body,
        [sent((n_y, 1 + cols, TILE, LANES), bf16)],
        (after(z_parts, from_near),),
        [vmem((n_y, 1 + cols, TILE, LANES), bf16)],
        sems=1,
    )
    y_parts = lax.all_to_all(y_out, "y", 0, 0, tiled=True)
    (hidden_grad,) = call(
        join_body,
        [sent((1, nodes, width), bf16)],
        (from_near, from_far),
        [vmem((nodes, width), bf16), vmem((2 * K, width), f32)],
        core=core_arg,
        hbm_args=(mid, edge),
        sems=3,
    )
    (last_out,) = call(
        sum_last_body,
        [sent((2 * MEMBERS, 1 + cols, TILE, LANES), bf16)],
        (after(y_parts, hidden_grad),),
        [vmem((1 + cols, TILE, LANES), bf16)],
        sems=2 * MEMBERS,
    )
    last = lax.all_to_all(last_out, ("mem", "core"), 0, 0, tiled=True)
    weight_grad, decoder_grad = call(
        final_body,
        [shape((TILE, width), f32), shape((variables, width), f32)],
        (last,),
        core=core_arg,
    )
    return (hidden_grad, weight_grad, decoder_grad.T)


def solution(mesh):
    members, blocks = mesh.shape["mem"], mesh.shape["grid"]
    split = jax.sharding.Mesh(mesh.devices.reshape(members, blocks // 8, 4, 2), ("mem",) + GRID)
    grid = GRID
    placed = (
        P("mem", grid, None),
        P("mem", None, grid),
        P(None, grid),
        P(grid),
        P(),
        P(grid),
        P(None, grid),
        P(None, grid),
        P(grid, None),
        P(),
    )
    return jax.shard_map(
        on_device,
        mesh=split,
        in_specs=placed,
        out_specs=(P("mem", grid, None), P(grid, None), P()),
        check_vma=False,
    )
```

```python
import math

import jax
import jax.numpy as jnp
from jax import lax
from jax.experimental import pallas as pl
from jax.experimental.pallas import tpu as pltpu
from jax.sharding import PartitionSpec as P

K = 64
KNB = 8
LANES = 128
TILE = 16
DEC_TILES = 4
MEMBERS = 8
GRID = ("z", "y", "core")
PAIR = ("z", "y")

norm_eps = 1e-05
alpha_fair = 0.95
root_half = 1.0 / math.sqrt(2.0)
inv_root_two_pi = 1.0 / math.sqrt(2.0 * math.pi)

f32 = jnp.float32
bf16 = jnp.bfloat16


def shape(dims, dtype):
    return jax.ShapeDtypeStruct(dims, dtype)


def dot(a, b, ca=1, cb=0):
    return lax.dot_general(a, b, (((ca,), (cb,)), ((), ())), preferred_element_type=f32)


class Copies:
    def __init__(self, sems):
        self.sems, self.used = sems, 0

    def start(self, src, dst):
        copy = pltpu.make_async_copy(src, dst, self.sems.at[self.used])
        self.used += 1
        copy.start()
        return copy


def after(x, *first):
    return lax.optimization_barrier((x,) + first)[0]


def sent(dims, dtype):
    return pltpu.HBM(dims, dtype)


def call(body, out, args, scratch=(), core=None, sems=0, hbm_args=(), flops=0, trans=0, mib=24):
    hbm_args = tuple(pltpu.with_memory_space_constraint(a, pltpu.HBM) for a in hbm_args)
    args = tuple(args) + hbm_args
    moved = sum(a.size * a.dtype.itemsize for a in args)
    moved += sum(math.prod(o.shape) * jnp.dtype(o.dtype).itemsize for o in out)
    first = [] if core is None else [core]

    def kernel(*refs):
        if sems:
            body(*refs[:-1], Copies(refs[-1]))
        else:
            body(*refs)

    vmem = pl.BlockSpec(memory_space=pltpu.VMEM)
    hbm = pl.BlockSpec(memory_space=pltpu.HBM)
    return pl.pallas_call(
        kernel,
        out_shape=out,
        in_specs=[pl.BlockSpec(memory_space=pltpu.SMEM)] * len(first) + [vmem] * (len(args) - len(hbm_args))
        + [hbm] * len(hbm_args),
        out_specs=[hbm if getattr(o, "memory_space", None) == pltpu.HBM else vmem for o in out],
        scratch_shapes=list(scratch) + ([pltpu.SemaphoreType.DMA((sems,))] if sems else []),
        cost_estimate=pl.CostEstimate(flops=flops, bytes_accessed=moved, transcendentals=trans),
        compiler_params=pltpu.CompilerParams(vmem_limit_bytes=mib * 2**20),
    )(*first, *args)


def packed(a):
    a = jnp.concatenate([a, jnp.zeros((7 * TILE - a.shape[0], a.shape[1]), f32)], axis=0)
    tail = a[:, 3 * LANES :]
    left = jnp.concatenate([tail[i * TILE : (i + 1) * TILE] for i in (0, 2, 4, 6)], axis=0)
    right = jnp.concatenate(
        [tail[i * TILE : (i + 1) * TILE] for i in (1, 3, 5)] + [jnp.zeros((TILE, LANES // 2), f32)], axis=0
    )
    return jnp.concatenate(
        [a[:, j * LANES : (j + 1) * LANES] for j in range(3)] + [jnp.concatenate([left, right], axis=1)], axis=0
    )


def unpacked(a, variables):
    last, half = a[21 * TILE :], LANES // 2
    tail = jnp.concatenate(
        [last[i // 2 * TILE : (i // 2 + 1) * TILE, (i % 2) * half : (i % 2 + 1) * half] for i in range(7)], axis=0
    )
    return jnp.concatenate([a[7 * j * TILE : 7 * (j + 1) * TILE] for j in range(3)] + [tail], axis=1)[0:variables]


def pack_body(pred_ref, out_hbm, wide_ref, copies):
    wide_ref[...] = packed(pred_ref[0].astype(f32)).astype(bf16).reshape(wide_ref.shape)
    for c in [copies.start(wide_ref, out_hbm.at[m]) for m in range(MEMBERS)]:
        c.wait()


def tile_body(pick_ref, own_ref, got_ref, out_hbm, out_ref, copies):
    tile = jnp.where(pick_ref[0] == 1, own_ref[...].astype(f32), got_ref[...].astype(f32)).astype(bf16)
    out_ref[...] = jnp.broadcast_to(tile[None], out_ref.shape)
    copies.start(out_ref, out_hbm).wait()


def edges_body(src_ref, ew_ref, at_hbm, at_ref, copies):
    rows, nodes = at_ref.shape
    for r in range(0, rows, K):
        j = lax.broadcasted_iota(jnp.int32, (K, nodes), 0) + r
        acc = jnp.zeros((K, nodes), f32)
        for s in range(KNB):
            acc += jnp.where(src_ref[s : s + 1, :] == j, ew_ref[s : s + 1, :], 0.0)
        at_ref[r : r + K, :] = acc.astype(bf16)
    copies.start(at_ref, at_hbm).wait()


def norm_body(
    core_ref, own_ref, near_ref, far_ref, at_hbm, rstd_hbm, keep_hbm, send_hbm, at_ref, li_ref, normed_ref, rstd_ref, copies
):
    copies.start(at_hbm, at_ref).wait()
    core = core_ref[0]
    nodes, width = own_ref.shape
    half = width // 2
    near_at = pl.multiple_of((1 - core) * (K + nodes), K)
    far_at = pl.multiple_of(core * (K + nodes), K)
    agg = dot(at_ref[pl.ds(near_at, K), :], near_ref[...], 0, 0)
    agg += dot(at_ref[K : K + nodes, :], own_ref[...], 0, 0)
    agg += dot(at_ref[pl.ds(far_at, K), :], far_ref[...], 0, 0)
    li = own_ref[...].astype(f32) + agg
    li_ref[...] = li.astype(bf16)
    mine = pl.multiple_of(core * half, half)
    theirs = pl.multiple_of((1 - core) * half, half)
    stores = [
        copies.start(li_ref.at[:, pl.ds(theirs, half)], send_hbm.at[:, pl.ds(width, half)]),
        copies.start(li_ref.at[:, pl.ds(mine, half)], keep_hbm),
    ]
    mean = jnp.mean(li, axis=-1, keepdims=True)
    dev = li - mean
    rstd = lax.rsqrt(jnp.mean(dev * dev, axis=-1, keepdims=True) + norm_eps)
    normed_ref[...] = (dev * rstd).astype(bf16)
    stores.append(copies.start(normed_ref, send_hbm.at[:, pl.ds(0, width)]))
    rstd_ref[...] = jnp.broadcast_to(rstd, rstd_ref.shape)
    stores.append(copies.start(rstd_ref, rstd_hbm))
    for c in stores:
        c.wait()


def pred_body(all_ref, own_ref, target_ref, lw_ref, out_ref):
    members = all_ref.shape[0]
    variables = out_ref.shape[0]
    coef_pair = (1.0 - (1.0 - alpha_fair) / members) / (members * (members - 1))

    def sign(a):
        return jnp.where(a > 0.0, 1.0, jnp.where(a < 0.0, -1.0, 0.0))

    own = packed(own_ref[0].astype(f32))
    pair_sum = jnp.zeros(own.shape, f32)
    for k in range(members):
        pair_sum += sign(own - all_ref[k].astype(f32).reshape(own.shape))
    to_target = sign(own_ref[0].astype(f32) - target_ref[...].astype(f32))
    pair_sum = unpacked(pair_sum, variables)
    out_ref[...] = (lw_ref[...] * (to_target / members - coef_pair * pair_sum)).astype(bf16)


def share_body(got_ref, out_hbm, copies):
    for c in [copies.start(got_ref, out_hbm.at[m]) for m in range(out_hbm.shape[0])]:
        c.wait()


def fill_weight(wg_ref, w_ref):
    cols = w_ref.shape[1] // LANES
    for g in range(wg_ref.shape[1]):
        for c in range(2):
            for x in range(cols):
                at = (2 * g + c) * TILE
                w_ref[at : at + TILE, x * LANES : (x + 1) * LANES] = wg_ref[c * cols + x, g]


def main_body(
    core_ref, wg_ref, own_hbm, keep_hbm, po_hbm, wd_hbm, got_hbm, pp_hbm, send_hbm, pre_hbm, ng_hbm,
    no_ref, keep_ref, po_ref, wd_ref, got_ref, pp_ref, w_ref, lo_ref, pre_ref, parts_ref, ng_ref, copies,
):
    core = core_ref[0]
    nodes, width = no_ref.shape
    half = width // 2
    cols = half // LANES
    pairs = parts_ref.shape[1] - cols
    loads = [
        [copies.start(own_hbm.at[:, pl.ds(0, width)], no_ref), copies.start(keep_hbm, keep_ref),
         copies.start(po_hbm, po_ref), copies.start(wd_hbm, wd_ref)],
        [copies.start(got_hbm, got_ref), copies.start(pp_hbm, pp_ref)],
    ]
    fill_weight(wg_ref, w_ref)
    stores = []
    for part in range(2):
        p_ref = (po_ref, pp_ref)[part]
        for c in loads[part]:
            c.wait()
        wd = wd_ref[:, pl.ds(pl.multiple_of(core * half, half), half)]
        for r in range(0, nodes, 128):
            step = min(128, nodes - r)
            n = no_ref[r : r + step, :] if part == 0 else got_ref[r : r + step, 0:width]
            li = keep_ref[r : r + step, :] if part == 0 else got_ref[r : r + step, width:]
            pre = dot(n, w_ref[...])
            og = dot(p_ref[:, r : r + step], wd, 0, 0)
            cdf = 0.5 * (1.0 + lax.erf(pre * root_half))
            pdf = jnp.exp(-0.5 * pre * pre) * inv_root_two_pi
            at = part * nodes + r
            lo_ref[at : at + step, :] = (li.astype(f32) + pre * cdf).astype(bf16)
            pre_ref[at : at + step, :] = (og * (cdf + pre * pdf)).astype(bf16)
    stores.append(copies.start(pre_ref.at[pl.ds(0, nodes)], pre_hbm))
    ng_ref[...] = dot(pre_ref[nodes:, :], w_ref[...], 1, 1).astype(bf16)
    stores.append(copies.start(ng_ref, ng_hbm))
    dec = dot(po_ref[...], lo_ref[0:nodes, :]) + dot(pp_ref[...], lo_ref[nodes:, :])
    dec = jnp.concatenate([dec, jnp.zeros((MEMBERS * TILE - dec.shape[0], half), f32)], axis=0).astype(bf16)
    for m in range(MEMBERS):
        for x in range(cols):
            parts_ref[m, pairs + x] = dec[m * TILE : (m + 1) * TILE, x * LANES : (x + 1) * LANES]
    rows = 256
    for q in range(0, width, rows):
        res = dot(no_ref[:, q : q + rows], pre_ref[0:nodes, :], 0, 0)
        res += dot(got_ref[:, q : q + rows], pre_ref[nodes:, :], 0, 0)
        res = res.astype(bf16)
        first, count = q // (2 * TILE), rows // (2 * TILE)
        for g in range(count):
            for c in range(2):
                for x in range(cols):
                    at = (2 * g + c) * TILE
                    parts_ref[c * cols + x, first + g] = res[at : at + TILE, x * LANES : (x + 1) * LANES]
        last = q + rows == width
        tiles = pl.ds(first, count + (cols if last else 0))
        stores.append(copies.start(parts_ref.at[:, tiles], send_hbm.at[:, tiles]))
    for c in stores:
        c.wait()


def scatter_body(
    core_ref, wg_ref, got_ref, rstd_hbm, po_hbm, wd_hbm, pre_hbm, own_hbm, at_hbm, mid_hbm, edge_hbm, near_ref, far_ref,
    w_ref, rstd_ref, po_ref, wd_ref, pre_ref, no_ref, at_ref, ib_ref, mid_ref, edge_ref, copies,
):
    core = core_ref[0]
    nodes, width = no_ref.shape
    first = copies.start(pre_hbm, pre_ref)
    loads = [
        copies.start(po_hbm, po_ref),
        copies.start(wd_hbm, wd_ref),
        copies.start(own_hbm.at[:, pl.ds(0, width)], no_ref),
        copies.start(rstd_hbm, rstd_ref),
        copies.start(at_hbm, at_ref),
    ]
    fill_weight(wg_ref, w_ref)
    first.wait()
    ng = dot(pre_ref[...], w_ref[...], 1, 1) + got_ref[...].astype(f32)
    for c in loads:
        c.wait()
    unit = no_ref[...].astype(f32)
    og = dot(po_ref[...], wd_ref[...], 0, 0)
    mean_g = jnp.mean(ng, axis=-1, keepdims=True)
    mean_c = jnp.mean(ng * unit, axis=-1, keepdims=True)
    ig = og + rstd_ref[:, 0:1] * (ng - mean_g - unit * mean_c)
    ib_ref[...] = ig.astype(bf16)
    near_at = pl.multiple_of((1 - core) * (K + nodes), K)
    far_at = pl.multiple_of(core * (K + nodes), K)
    near_ref[...] = dot(at_ref[pl.ds(near_at, K), :], ib_ref[...]).astype(bf16)
    far_ref[...] = dot(at_ref[pl.ds(far_at, K), :], ib_ref[...]).astype(bf16)
    total = ig + dot(at_ref[K : K + nodes, :], ib_ref[...])
    mid_ref[...] = total.astype(bf16)
    edge_ref[0:K, :] = total[0:K, :]
    edge_ref[K:, :] = total[nodes - K :, :]
    for c in [copies.start(mid_ref, mid_hbm), copies.start(edge_ref, edge_hbm)]:
        c.wait()


def join_body(core_ref, near_ref, far_ref, mid_hbm, edge_hbm, out_hbm, mid_ref, edge_ref, copies):
    core = core_ref[0]
    nodes = mid_ref.shape[0]
    loads = [copies.start(mid_hbm, mid_ref), copies.start(edge_hbm, edge_ref)]
    for c in loads:
        c.wait()
    for ref, end in ((near_ref, 1 - core), (far_ref, core)):
        edge = edge_ref[pl.ds(pl.multiple_of(end * K, K), K), :] + ref[...].astype(f32)
        mid_ref[pl.ds(pl.multiple_of(end * (nodes - K), K), K), :] = edge.astype(bf16)
    copies.start(mid_ref, out_hbm.at[0]).wait()


def total_of(got_ref):
    total = got_ref[0].astype(f32)
    for i in range(1, got_ref.shape[0]):
        total += got_ref[i].astype(f32)
    return total.astype(bf16)


def sum_body(got_ref, out_hbm, out_ref, copies):
    total = total_of(got_ref)
    parts, tiles = out_ref.shape[:2]
    dec = DEC_TILES
    weights = got_ref.shape[1] - dec
    each = weights // parts
    out_ref[:, 0:each] = total[0:weights].reshape(parts, each, TILE, LANES)
    out_ref[:, each:] = jnp.broadcast_to(total[weights:][None], (parts, dec, TILE, LANES))
    copies.start(out_ref, out_hbm).wait()


def sum_last_body(got_ref, out_hbm, out_ref, copies):
    out_ref[...] = total_of(got_ref)
    for c in [copies.start(out_ref, out_hbm.at[m]) for m in range(out_hbm.shape[0])]:
        c.wait()


def final_body(core_ref, got_ref, weight_ref, dec_ref):
    core = core_ref[0]
    half = weight_ref.shape[1] // 2
    cols = half // LANES
    variables = dec_ref.shape[0]
    for c in range(2):
        for x in range(cols):
            lane = c * half + x * LANES
            weight_ref[:, lane : lane + LANES] = got_ref[(core * cols + x) * 2 + c, 0].astype(f32)
            for m in range(MEMBERS):
                rows = min(TILE, variables - m * TILE)
                if rows > 0:
                    tile = got_ref[m * 2 + c, 1 + x].astype(f32)
                    dec_ref[m * TILE : m * TILE + rows, lane : lane + LANES] = tile[0:rows, :]


def other_pair(a):
    size = lax.axis_size(GRID)
    pairs = [(i, i + (1 if i % 2 else -1)) for i in range(1, size - 1)]
    return lax.ppermute(a, GRID, pairs)


def other_core(a):
    return lax.ppermute(a, "core", [(0, 1), (1, 0)])


def over_pairs(a):
    return lax.all_to_all(a, PAIR, 0, 0, tiled=True)


def over_mem(a):
    return lax.all_to_all(a, "mem", 0, 0, tiled=True)


def on_device(
    hidden, predictions, target, area, var_weight, interior, sources, edge_weight, w_node, w_dec
):
    pairs = lax.axis_size(PAIR)
    nodes, width = hidden.shape[1:]
    half = width // 2
    cols = half // LANES
    variables = w_dec.shape[1]
    rows = -(-variables // TILE) * TILE
    core = lax.axis_index("core")
    member = lax.axis_index("mem")
    core_arg = core.astype(jnp.int32).reshape(1)
    own = hidden[0]
    vmem = pltpu.VMEM

    row_half, col_block = member // cols, member % cols
    tile_own = lax.dynamic_slice(w_node, (0, core * half + col_block * LANES), (TILE, LANES))
    tile_out = lax.dynamic_slice(w_node, (0, (1 - core) * half + col_block * LANES), (TILE, LANES))
    tile_got = other_core(tile_out)
    own_half = (core == row_half).astype(jnp.int32).reshape(1)
    (tiles,) = call(
        tile_body,
        [sent((pairs, TILE, LANES), bf16)],
        (tile_own, tile_got),
        [vmem((pairs, TILE, LANES), bf16)],
        core=own_half,
        sems=1,
    )

    (spread_pred,) = call(
        pack_body,
        [sent((MEMBERS, 25, TILE, LANES), bf16)],
        (predictions,),
        [vmem((25, TILE, LANES), bf16)],
        sems=MEMBERS,
    )
    every_pred = over_mem(spread_pred)
    near = other_core(lax.dynamic_slice(own, ((1 - core) * (nodes - K), 0), (K, width)))
    far = other_pair(lax.dynamic_slice(own, (core * (nodes - K), 0), (K, width)))
    (at,) = call(
        edges_body, [sent((nodes + 2 * K, nodes), bf16)], (sources, edge_weight),
        [vmem((nodes + 2 * K, nodes), bf16)], sems=1,
    )
    shards = over_pairs(after(tiles, every_pred))
    rstd, keep, send = call(
        norm_body,
        [sent((nodes, LANES), f32), sent((nodes, half), bf16), sent((nodes, width + half), bf16)],
        (after(own, shards), near, far),
        [vmem((nodes + 2 * K, nodes), bf16), vmem((nodes, width), bf16), vmem((nodes, width), bf16),
         vmem((nodes, LANES), f32)],
        core=core_arg,
        hbm_args=(at,),
        sems=5,
        flops=2 * nodes * (nodes + 2 * K) * width,
    )
    got = other_core(send)
    loss_weight = var_weight[:, None] * (area * interior.astype(f32))[None, :]
    (pred_grad,) = call(
        pred_body,
        [shape((variables, nodes), bf16)],
        (every_pred, predictions, target, loss_weight),
    )
    pred_got = other_core(pred_grad)
    dec_t = w_dec.T

    (spread,) = call(
        share_body,
        [sent((MEMBERS, pairs, TILE, LANES), bf16)],
        (after(shards, pred_got, near, far, at),),
        sems=MEMBERS,
    )
    weight = over_mem(spread)

    weight_shape = vmem((width, half), bf16)
    part_shape = (MEMBERS, pairs + cols, TILE, LANES)
    parts, pre_grad, ng_send = call(
        main_body,
        [sent(part_shape, bf16), sent((nodes, half), bf16), sent((nodes, width), bf16)],
        (weight,),
        [vmem((nodes, width), bf16), vmem((nodes, half), bf16), vmem((variables, nodes), bf16),
         vmem((variables, width), bf16), vmem((nodes, width + half), bf16), vmem((variables, nodes), bf16), weight_shape, vmem((2 * nodes, half), bf16),
         vmem((2 * nodes, half), bf16), vmem(part_shape, bf16), vmem((nodes, width), bf16)],
        core=core_arg,
        hbm_args=(send, keep, pred_grad, dec_t, got, pred_got),
        sems=16,
        flops=5 * 2 * nodes * width * half,
        trans=4 * nodes * half,
    )
    mem_parts = over_mem(parts)

    ng_got = other_core(ng_send)
    mid, edge, to_near, to_far = call(
        scatter_body,
        [sent((nodes, width), bf16), sent((2 * K, width), f32), shape((K, width), bf16), shape((K, width), bf16)],
        (weight, ng_got),
        [weight_shape, vmem((nodes, LANES), f32), vmem((variables, nodes), bf16), vmem((variables, width), bf16),
         vmem((nodes, half), bf16), vmem((nodes, width), bf16), vmem((nodes + 2 * K, nodes), bf16),
         vmem((nodes, width), bf16), vmem((nodes, width), bf16), vmem((2 * K, width), f32)],
        core=core_arg,
        hbm_args=(rstd, pred_grad, dec_t, pre_grad, send, at),
        sems=8,
        flops=2 * nodes * (nodes + 2 * K) * width,
    )
    from_near = other_core(to_near)
    from_far = other_pair(to_far)
    n_z, n_y = lax.axis_size("z"), lax.axis_size("y")
    (z_out,) = call(
        sum_body,
        [sent((n_z, n_y + cols, TILE, LANES), bf16)],
        (after(mem_parts, to_near),),
        [vmem((n_z, n_y + cols, TILE, LANES), bf16)],
        sems=1,
    )
    z_parts = lax.all_to_all(z_out, "z", 0, 0, tiled=True)
    (y_out,) = call(
        sum_body,
        [sent((n_y, 1 + cols, TILE, LANES), bf16)],
        (after(z_parts, from_near),),
        [vmem((n_y, 1 + cols, TILE, LANES), bf16)],
        sems=1,
    )
    y_parts = lax.all_to_all(y_out, "y", 0, 0, tiled=True)
    (hidden_grad,) = call(
        join_body,
        [sent((1, nodes, width), bf16)],
        (from_near, from_far),
        [vmem((nodes, width), bf16), vmem((2 * K, width), f32)],
        core=core_arg,
        hbm_args=(mid, edge),
        sems=3,
    )
    (last_out,) = call(
        sum_last_body,
        [sent((2 * MEMBERS, 1 + cols, TILE, LANES), bf16)],
        (after(y_parts, hidden_grad),),
        [vmem((1 + cols, TILE, LANES), bf16)],
        sems=2 * MEMBERS,
    )
    last = lax.all_to_all(last_out, ("mem", "core"), 0, 0, tiled=True)
    weight_grad, decoder_grad = call(
        final_body,
        [shape((TILE, width), f32), shape((variables, width), f32)],
        (last,),
        core=core_arg,
    )
    return (hidden_grad, weight_grad, decoder_grad.T)


def solution(mesh):
    members, blocks = mesh.shape["mem"], mesh.shape["grid"]
    split = jax.sharding.Mesh(mesh.devices.reshape(members, blocks // 8, 4, 2), ("mem",) + GRID)
    grid = GRID
    placed = (
        P("mem", grid, None),
        P("mem", None, grid),
        P(None, grid),
        P(grid),
        P(),
        P(grid),
        P(None, grid),
        P(None, grid),
        P(grid, None),
        P(),
    )
    return jax.shard_map(
        on_device,
        mesh=split,
        in_specs=placed,
        out_specs=(P("mem", grid, None), P(grid, None), P()),
        check_vma=False,
    )
```

```python
import math

import jax
import jax.numpy as jnp
from jax import lax
from jax.experimental import pallas as pl
from jax.experimental.pallas import tpu as pltpu
from jax.sharding import PartitionSpec as P

K = 64
KNB = 8
LANES = 128
TILE = 16
DEC_TILES = 4
MEMBERS = 8
GRID = ("z", "y", "core")
PAIR = ("z", "y")

norm_eps = 1e-05
alpha_fair = 0.95
root_half = 1.0 / math.sqrt(2.0)
inv_root_two_pi = 1.0 / math.sqrt(2.0 * math.pi)

f32 = jnp.float32
bf16 = jnp.bfloat16


def shape(dims, dtype):
    return jax.ShapeDtypeStruct(dims, dtype)


def dot(a, b, ca=1, cb=0):
    return lax.dot_general(a, b, (((ca,), (cb,)), ((), ())), preferred_element_type=f32)


class Copies:
    def __init__(self, sems):
        self.sems, self.used = sems, 0

    def start(self, src, dst):
        copy = pltpu.make_async_copy(src, dst, self.sems.at[self.used])
        self.used += 1
        copy.start()
        return copy


def after(x, *first):
    return lax.optimization_barrier((x,) + first)[0]


def sent(dims, dtype):
    return pltpu.HBM(dims, dtype)


def staged(dims, dtype):
    return pltpu.VMEM(dims, dtype)


def call(body, out, args, scratch=(), core=None, sems=0, hbm_args=(), flops=0, trans=0, mib=24):
    hbm_args = tuple(pltpu.with_memory_space_constraint(a, pltpu.HBM) for a in hbm_args)
    args = tuple(args) + hbm_args
    moved = sum(a.size * a.dtype.itemsize for a in args)
    moved += sum(math.prod(o.shape) * jnp.dtype(o.dtype).itemsize for o in out)
    first = [] if core is None else [core]

    def kernel(*refs):
        if sems:
            body(*refs[:-1], Copies(refs[-1]))
        else:
            body(*refs)

    vmem = pl.BlockSpec(memory_space=pltpu.VMEM)
    hbm = pl.BlockSpec(memory_space=pltpu.HBM)
    return pl.pallas_call(
        kernel,
        out_shape=out,
        in_specs=[pl.BlockSpec(memory_space=pltpu.SMEM)] * len(first) + [vmem] * (len(args) - len(hbm_args))
        + [hbm] * len(hbm_args),
        out_specs=[hbm if getattr(o, "memory_space", None) == pltpu.HBM else vmem for o in out],
        scratch_shapes=list(scratch) + ([pltpu.SemaphoreType.DMA((sems,))] if sems else []),
        cost_estimate=pl.CostEstimate(flops=flops, bytes_accessed=moved, transcendentals=trans),
        compiler_params=pltpu.CompilerParams(vmem_limit_bytes=mib * 2**20),
    )(*first, *args)


def packed(a):
    rows, half = a.shape[0], a.shape[0] // 2
    tail = a[:, 3 * LANES :]
    parts = [a[:, j * LANES : (j + 1) * LANES] for j in range(3)]
    parts.append(jnp.concatenate([tail[0:half], tail[half:]], axis=1))
    fill = -(3 * rows + half) % TILE
    if fill:
        parts.append(jnp.zeros((fill, LANES), f32))
    return jnp.concatenate(parts, axis=0)


def unpacked(a, rows):
    half = rows // 2
    last = a[3 * rows : 3 * rows + half]
    tail = jnp.concatenate([last[:, 0 : LANES // 2], last[:, LANES // 2 :]], axis=0)
    return jnp.concatenate([a[j * rows : (j + 1) * rows] for j in range(3)] + [tail], axis=1)


def pack_body(pred_ref, out_hbm, wide_ref, copies):
    wide_ref[...] = packed(pred_ref[0].astype(f32)).astype(bf16).reshape(wide_ref.shape)
    for c in [copies.start(wide_ref, out_hbm.at[m]) for m in range(MEMBERS)]:
        c.wait()


def tile_body(pick_ref, own_ref, got_ref, out_hbm, out_ref, copies):
    at = pl.ds(pl.multiple_of(pick_ref[1] * LANES, LANES), LANES)
    own, got = own_ref[:, at].astype(f32), got_ref[K:, at].astype(f32)
    tile = jnp.where(pick_ref[0] == 1, own, got).astype(bf16)
    out_ref[...] = jnp.broadcast_to(tile[None], out_ref.shape)
    copies.start(out_ref, out_hbm).wait()


def edges_body(src_ref, ew_ref, at_hbm, at_ref, copies):
    rows, nodes = at_ref.shape
    for r in range(0, rows, K):
        j = lax.broadcasted_iota(jnp.int32, (K, nodes), 0) + r
        acc = jnp.zeros((K, nodes), f32)
        for s in range(KNB):
            acc += jnp.where(src_ref[s : s + 1, :] == j, ew_ref[s : s + 1, :], 0.0)
        at_ref[r : r + K, :] = acc.astype(bf16)
    copies.start(at_ref, at_hbm).wait()


def norm_body(
    core_ref, own_ref, near_ref, far_ref, at_hbm, rstd_hbm, keep_hbm, normed_ref, send_hbm, at_ref, li_ref, rstd_ref, copies
):
    copies.start(at_hbm, at_ref).wait()
    core = core_ref[0]
    nodes, width = own_ref.shape
    half = width // 2
    near_at = pl.multiple_of((1 - core) * (K + nodes), K)
    far_at = pl.multiple_of(core * (K + nodes), K)
    agg = dot(at_ref[pl.ds(near_at, K), :], near_ref[0:K, :], 0, 0)
    agg += dot(at_ref[K : K + nodes, :], own_ref[...], 0, 0)
    agg += dot(at_ref[pl.ds(far_at, K), :], far_ref[...], 0, 0)
    li = own_ref[...].astype(f32) + agg
    li_ref[...] = li.astype(bf16)
    mine = pl.multiple_of(core * half, half)
    theirs = pl.multiple_of((1 - core) * half, half)
    stores = [
        copies.start(li_ref.at[:, pl.ds(theirs, half)], send_hbm.at[:, pl.ds(width, half)]),
        copies.start(li_ref.at[:, pl.ds(mine, half)], keep_hbm),
    ]
    mean = jnp.mean(li, axis=-1, keepdims=True)
    dev = li - mean
    rstd = lax.rsqrt(jnp.mean(dev * dev, axis=-1, keepdims=True) + norm_eps)
    normed_ref[...] = (dev * rstd).astype(bf16)
    stores.append(copies.start(normed_ref, send_hbm.at[:, pl.ds(0, width)]))
    rstd_ref[...] = jnp.broadcast_to(rstd, rstd_ref.shape)
    stores.append(copies.start(rstd_ref, rstd_hbm))
    for c in stores:
        c.wait()


def pred_body(all_ref, own_ref, target_ref, lw_ref, out_ref):
    members = all_ref.shape[0]
    variables = out_ref.shape[0]
    coef_pair = (1.0 - (1.0 - alpha_fair) / members) / (members * (members - 1))

    def sign(a):
        return jnp.where(a > 0.0, 1.0, jnp.where(a < 0.0, -1.0, 0.0))

    own = packed(own_ref[0].astype(f32))
    pair_sum = jnp.zeros(own.shape, f32)
    for k in range(members):
        pair_sum += sign(own - all_ref[k].astype(f32).reshape(own.shape))
    to_target = sign(own_ref[0].astype(f32) - target_ref[...].astype(f32))
    pair_sum = unpacked(pair_sum, variables)
    out_ref[...] = (lw_ref[...] * (to_target / members - coef_pair * pair_sum)).astype(bf16)


def share_body(got_ref, out_hbm, copies):
    for c in [copies.start(got_ref, out_hbm.at[m]) for m in range(out_hbm.shape[0])]:
        c.wait()


def fill_weight(wg_ref, w_ref):
    cols = w_ref.shape[1] // LANES
    for g in range(wg_ref.shape[1]):
        for c in range(2):
            for x in range(cols):
                at = (2 * g + c) * TILE
                w_ref[at : at + TILE, x * LANES : (x + 1) * LANES] = wg_ref[c * cols + x, g]


def main_body(
    core_ref, wg_ref, no_ref, keep_hbm, po_hbm, wd_hbm, got_hbm, pp_hbm, send_hbm, pre_hbm, ng_hbm,
    keep_ref, po_ref, wd_ref, got_ref, pp_ref, w_ref, lo_ref, pre_ref, parts_ref, ng_ref, copies,
):
    core = core_ref[0]
    nodes, width = no_ref.shape
    half = width // 2
    cols = half // LANES
    pairs = parts_ref.shape[1] - cols
    loads = [
        [copies.start(po_hbm, po_ref), copies.start(wd_hbm, wd_ref), copies.start(keep_hbm, keep_ref)],
        [copies.start(got_hbm, got_ref), copies.start(pp_hbm, pp_ref)],
    ]
    fill_weight(wg_ref, w_ref)
    stores = []
    for part in range(2):
        p_ref = (po_ref, pp_ref)[part]
        for c in loads[part]:
            c.wait()
        wd = wd_ref[:, pl.ds(pl.multiple_of(core * half, half), half)]
        for r in range(0, nodes, 128):
            step = min(128, nodes - r)
            n = no_ref[r : r + step, :] if part == 0 else got_ref[r : r + step, 0:width]
            li = keep_ref[r : r + step, :] if part == 0 else got_ref[r : r + step, width:]
            pre = dot(n, w_ref[...])
            og = dot(p_ref[:, r : r + step], wd, 0, 0)
            cdf = 0.5 * (1.0 + lax.erf(pre * root_half))
            pdf = jnp.exp(-0.5 * pre * pre) * inv_root_two_pi
            at = part * nodes + r
            lo_ref[at : at + step, :] = (li.astype(f32) + pre * cdf).astype(bf16)
            pre_ref[at : at + step, :] = (og * (cdf + pre * pdf)).astype(bf16)
    stores.append(copies.start(pre_ref.at[pl.ds(0, nodes)], pre_hbm))
    ng_ref[...] = dot(pre_ref[nodes:, :], w_ref[...], 1, 1).astype(bf16)
    stores.append(copies.start(ng_ref, ng_hbm))
    dec = dot(po_ref[...], lo_ref[0:nodes, :]) + dot(pp_ref[...], lo_ref[nodes:, :])
    dec = jnp.concatenate([dec, jnp.zeros((MEMBERS * TILE - dec.shape[0], half), f32)], axis=0).astype(bf16)
    for m in range(MEMBERS):
        for x in range(cols):
            parts_ref[m, pairs + x] = dec[m * TILE : (m + 1) * TILE, x * LANES : (x + 1) * LANES]
    rows = 256
    for q in range(0, width, rows):
        res = dot(no_ref[:, q : q + rows], pre_ref[0:nodes, :], 0, 0)
        res += dot(got_ref[:, q : q + rows], pre_ref[nodes:, :], 0, 0)
        res = res.astype(bf16)
        first, count = q // (2 * TILE), rows // (2 * TILE)
        for g in range(count):
            for c in range(2):
                for x in range(cols):
                    at = (2 * g + c) * TILE
                    parts_ref[c * cols + x, first + g] = res[at : at + TILE, x * LANES : (x + 1) * LANES]
        last = q + rows == width
        tiles = pl.ds(first, count + (cols if last else 0))
        stores.append(copies.start(parts_ref.at[:, tiles], send_hbm.at[:, tiles]))
    for c in stores:
        c.wait()


def scatter_body(
    core_ref, wg_ref, got_ref, rstd_hbm, po_hbm, wd_hbm, pre_hbm, own_hbm, at_hbm, mid_hbm, edge_hbm, near_ref, far_ref,
    w_ref, rstd_ref, po_ref, wd_ref, pre_ref, no_ref, at_ref, ib_ref, mid_ref, edge_ref, copies,
):
    core = core_ref[0]
    nodes, width = no_ref.shape
    first = copies.start(pre_hbm, pre_ref)
    loads = [
        copies.start(po_hbm, po_ref),
        copies.start(wd_hbm, wd_ref),
        copies.start(own_hbm.at[:, pl.ds(0, width)], no_ref),
        copies.start(rstd_hbm, rstd_ref),
        copies.start(at_hbm, at_ref),
    ]
    fill_weight(wg_ref, w_ref)
    first.wait()
    ng = dot(pre_ref[...], w_ref[...], 1, 1) + got_ref[...].astype(f32)
    for c in loads:
        c.wait()
    unit = no_ref[...].astype(f32)
    og = dot(po_ref[...], wd_ref[...], 0, 0)
    mean_g = jnp.mean(ng, axis=-1, keepdims=True)
    mean_c = jnp.mean(ng * unit, axis=-1, keepdims=True)
    ig = og + rstd_ref[:, 0:1] * (ng - mean_g - unit * mean_c)
    ib_ref[...] = ig.astype(bf16)
    near_at = pl.multiple_of((1 - core) * (K + nodes), K)
    far_at = pl.multiple_of(core * (K + nodes), K)
    near_ref[...] = dot(at_ref[pl.ds(near_at, K), :], ib_ref[...]).astype(bf16)
    far_ref[...] = dot(at_ref[pl.ds(far_at, K), :], ib_ref[...]).astype(bf16)
    total = ig + dot(at_ref[K : K + nodes, :], ib_ref[...])
    mid_ref[...] = total.astype(bf16)
    edge_ref[0:K, :] = total[0:K, :]
    edge_ref[K:, :] = total[nodes - K :, :]
    for c in [copies.start(mid_ref, mid_hbm), copies.start(edge_ref, edge_hbm)]:
        c.wait()


def join_body(core_ref, near_ref, far_ref, mid_hbm, edge_hbm, out_hbm, mid_ref, edge_ref, copies):
    core = core_ref[0]
    nodes = mid_ref.shape[0]
    loads = [copies.start(mid_hbm, mid_ref), copies.start(edge_hbm, edge_ref)]
    for c in loads:
        c.wait()
    for ref, end in ((near_ref, 1 - core), (far_ref, core)):
        edge = edge_ref[pl.ds(pl.multiple_of(end * K, K), K), :] + ref[...].astype(f32)
        mid_ref[pl.ds(pl.multiple_of(end * (nodes - K), K), K), :] = edge.astype(bf16)
    copies.start(mid_ref, out_hbm.at[0]).wait()


def total_of(got_ref):
    total = got_ref[0].astype(f32)
    for i in range(1, got_ref.shape[0]):
        total += got_ref[i].astype(f32)
    return total.astype(bf16)


def sum_body(got_ref, out_hbm, out_ref, copies):
    total = total_of(got_ref)
    parts, tiles = out_ref.shape[:2]
    dec = DEC_TILES
    weights = got_ref.shape[1] - dec
    each = weights // parts
    out_ref[:, 0:each] = total[0:weights].reshape(parts, each, TILE, LANES)
    out_ref[:, each:] = jnp.broadcast_to(total[weights:][None], (parts, dec, TILE, LANES))
    copies.start(out_ref, out_hbm).wait()


def sum_last_body(got_ref, out_hbm, out_ref, copies):
    out_ref[...] = total_of(got_ref)
    for c in [copies.start(out_ref, out_hbm.at[m]) for m in range(out_hbm.shape[0])]:
        c.wait()


def final_body(core_ref, got_ref, weight_ref, dec_ref):
    core = core_ref[0]
    half = weight_ref.shape[1] // 2
    cols = half // LANES
    variables = dec_ref.shape[0]
    for c in range(2):
        for x in range(cols):
            lane = c * half + x * LANES
            weight_ref[:, lane : lane + LANES] = got_ref[(core * cols + x) * 2 + c, 0].astype(f32)
            for m in range(MEMBERS):
                rows = min(TILE, variables - m * TILE)
                if rows > 0:
                    tile = got_ref[m * 2 + c, 1 + x].astype(f32)
                    dec_ref[m * TILE : m * TILE + rows, lane : lane + LANES] = tile[0:rows, :]


def other_pair(a):
    size = lax.axis_size(GRID)
    pairs = [(i, i + (1 if i % 2 else -1)) for i in range(1, size - 1)]
    return lax.ppermute(a, GRID, pairs)


def other_core(a):
    return lax.ppermute(a, "core", [(0, 1), (1, 0)])


def over_pairs(a):
    return lax.all_to_all(a, PAIR, 0, 0, tiled=True)


def over_mem(a):
    return lax.all_to_all(a, "mem", 0, 0, tiled=True)


def on_device(
    hidden, predictions, target, area, var_weight, interior, sources, edge_weight, w_node, w_dec
):
    pairs = lax.axis_size(PAIR)
    nodes, width = hidden.shape[1:]
    half = width // 2
    cols = half // LANES
    variables = w_dec.shape[1]
    rows = -(-variables // TILE) * TILE
    core = lax.axis_index("core")
    member = lax.axis_index("mem")
    core_arg = core.astype(jnp.int32).reshape(1)
    own = hidden[0]
    vmem = pltpu.VMEM

    row_half, col_block = member // cols, member % cols
    edge = lax.dynamic_slice(own, ((1 - core) * (nodes - K), 0), (K, width))
    near = other_core(jnp.concatenate([edge, w_node]))
    pick = jnp.stack([(core == row_half).astype(jnp.int32), (core * cols + col_block).astype(jnp.int32)])
    (tiles,) = call(
        tile_body,
        [sent((pairs, TILE, LANES), bf16)],
        (w_node, near),
        [vmem((pairs, TILE, LANES), bf16)],
        core=pick,
        sems=1,
    )

    pred_tiles = -(-variables * nodes // (TILE * LANES))
    (spread_pred,) = call(
        pack_body,
        [sent((MEMBERS, pred_tiles, TILE, LANES), bf16)],
        (predictions,),
        [vmem((pred_tiles, TILE, LANES), bf16)],
        sems=MEMBERS,
    )
    every_pred = over_mem(spread_pred)
    far = other_pair(lax.dynamic_slice(own, (core * (nodes - K), 0), (K, width)))
    (at,) = call(
        edges_body, [sent((nodes + 2 * K, nodes), bf16)], (sources, edge_weight),
        [vmem((nodes + 2 * K, nodes), bf16)], sems=1,
    )
    shards = over_pairs(after(tiles, every_pred))
    rstd, keep, normed, send = call(
        norm_body,
        [sent((nodes, LANES), f32), sent((nodes, half), bf16), staged((nodes, width), bf16),
         sent((nodes, width + half), bf16)],
        (after(own, shards), near, far),
        [vmem((nodes + 2 * K, nodes), bf16), vmem((nodes, width), bf16), vmem((nodes, LANES), f32)],
        core=core_arg,
        hbm_args=(at,),
        sems=5,
        flops=2 * nodes * (nodes + 2 * K) * width,
    )
    got = other_core(send)
    loss_weight = var_weight[:, None] * (area * interior.astype(f32))[None, :]
    (pred_grad,) = call(
        pred_body,
        [shape((variables, nodes), bf16)],
        (every_pred, predictions, target, loss_weight),
    )
    pred_got = other_core(pred_grad)
    dec_t = w_dec.T

    (spread,) = call(
        share_body,
        [sent((MEMBERS, pairs, TILE, LANES), bf16)],
        (after(shards, pred_got, far, at),),
        sems=MEMBERS,
    )
    weight = over_mem(spread)

    weight_shape = vmem((width, half), bf16)
    part_shape = (MEMBERS, pairs + cols, TILE, LANES)
    parts, pre_grad, ng_send = call(
        main_body,
        [sent(part_shape, bf16), sent((nodes, half), bf16), sent((nodes, width), bf16)],
        (weight, normed),
        [vmem((nodes, half), bf16), vmem((variables, nodes), bf16),
         vmem((variables, width), bf16), vmem((nodes, width + half), bf16), vmem((variables, nodes), bf16), weight_shape, vmem((2 * nodes, half), bf16),
         vmem((2 * nodes, half), bf16), vmem(part_shape, bf16), vmem((nodes, width), bf16)],
        core=core_arg,
        hbm_args=(keep, pred_grad, dec_t, got, pred_got),
        sems=16,
        flops=5 * 2 * nodes * width * half,
        trans=4 * nodes * half,
    )
    mem_parts = over_mem(parts)

    ng_got = other_core(ng_send)
    mid, edge, to_near, to_far = call(
        scatter_body,
        [sent((nodes, width), bf16), sent((2 * K, width), f32), shape((K, width), bf16), shape((K, width), bf16)],
        (weight, ng_got),
        [weight_shape, vmem((nodes, LANES), f32), vmem((variables, nodes), bf16), vmem((variables, width), bf16),
         vmem((nodes, half), bf16), vmem((nodes, width), bf16), vmem((nodes + 2 * K, nodes), bf16),
         vmem((nodes, width), bf16), vmem((nodes, width), bf16), vmem((2 * K, width), f32)],
        core=core_arg,
        hbm_args=(rstd, pred_grad, dec_t, pre_grad, send, at),
        sems=8,
        flops=2 * nodes * (nodes + 2 * K) * width,
    )
    from_near = other_core(to_near)
    from_far = other_pair(to_far)
    n_z, n_y = lax.axis_size("z"), lax.axis_size("y")
    (z_out,) = call(
        sum_body,
        [sent((n_z, n_y + cols, TILE, LANES), bf16)],
        (after(mem_parts, to_near),),
        [vmem((n_z, n_y + cols, TILE, LANES), bf16)],
        sems=1,
    )
    z_parts = lax.all_to_all(z_out, "z", 0, 0, tiled=True)
    (y_out,) = call(
        sum_body,
        [sent((n_y, 1 + cols, TILE, LANES), bf16)],
        (after(z_parts, from_near),),
        [vmem((n_y, 1 + cols, TILE, LANES), bf16)],
        sems=1,
    )
    y_parts = lax.all_to_all(y_out, "y", 0, 0, tiled=True)
    (hidden_grad,) = call(
        join_body,
        [sent((1, nodes, width), bf16)],
        (from_near, from_far),
        [vmem((nodes, width), bf16), vmem((2 * K, width), f32)],
        core=core_arg,
        hbm_args=(mid, edge),
        sems=3,
    )
    (last_out,) = call(
        sum_last_body,
        [sent((2 * MEMBERS, 1 + cols, TILE, LANES), bf16)],
        (after(y_parts, hidden_grad),),
        [vmem((1 + cols, TILE, LANES), bf16)],
        sems=2 * MEMBERS,
    )
    last = lax.all_to_all(last_out, ("mem", "core"), 0, 0, tiled=True)
    weight_grad, decoder_grad = call(
        final_body,
        [shape((TILE, width), f32), shape((variables, width), f32)],
        (last,),
        core=core_arg,
    )
    return (hidden_grad, weight_grad, decoder_grad.T)


def solution(mesh):
    members, blocks = mesh.shape["mem"], mesh.shape["grid"]
    split = jax.sharding.Mesh(mesh.devices.reshape(members, blocks // 8, 4, 2), ("mem",) + GRID)
    grid = GRID
    placed = (
        P("mem", grid, None),
        P("mem", None, grid),
        P(None, grid),
        P(grid),
        P(),
        P(grid),
        P(None, grid),
        P(None, grid),
        P(grid, None),
        P(),
    )
    return jax.shard_map(
        on_device,
        mesh=split,
        in_specs=placed,
        out_specs=(P("mem", grid, None), P(grid, None), P()),
        check_vma=False,
    )
```

```python
import math

import jax
import jax.numpy as jnp
from jax import lax
from jax.experimental import pallas as pl
from jax.experimental.pallas import tpu as pltpu
from jax.sharding import PartitionSpec as P

K = 64
KNB = 8
LANES = 128
TILE = 16
DEC_TILES = 4
MEMBERS = 8
GRID = ("z", "y", "core")
PAIR = ("z", "y")

norm_eps = 1e-05
alpha_fair = 0.95
root_half = 1.0 / math.sqrt(2.0)
inv_root_two_pi = 1.0 / math.sqrt(2.0 * math.pi)

f32 = jnp.float32
bf16 = jnp.bfloat16


def shape(dims, dtype):
    return jax.ShapeDtypeStruct(dims, dtype)


def dot(a, b, ca=1, cb=0):
    return lax.dot_general(a, b, (((ca,), (cb,)), ((), ())), preferred_element_type=f32)


class Copies:
    def __init__(self, sems):
        self.sems, self.used = sems, 0

    def start(self, src, dst):
        copy = pltpu.make_async_copy(src, dst, self.sems.at[self.used])
        self.used += 1
        copy.start()
        return copy


def after(x, *first):
    return lax.optimization_barrier((x,) + first)[0]


def sent(dims, dtype):
    return pltpu.HBM(dims, dtype)


def staged(dims, dtype):
    return pltpu.VMEM(dims, dtype)


def call(body, out, args, scratch=(), core=None, sems=0, hbm_args=(), flops=0, trans=0, mib=24):
    hbm_args = tuple(pltpu.with_memory_space_constraint(a, pltpu.HBM) for a in hbm_args)
    args = tuple(args) + hbm_args
    moved = sum(a.size * a.dtype.itemsize for a in args)
    moved += sum(math.prod(o.shape) * jnp.dtype(o.dtype).itemsize for o in out)
    first = [] if core is None else [core]

    def kernel(*refs):
        if sems:
            body(*refs[:-1], Copies(refs[-1]))
        else:
            body(*refs)

    vmem = pl.BlockSpec(memory_space=pltpu.VMEM)
    hbm = pl.BlockSpec(memory_space=pltpu.HBM)
    return pl.pallas_call(
        kernel,
        out_shape=out,
        in_specs=[pl.BlockSpec(memory_space=pltpu.SMEM)] * len(first) + [vmem] * (len(args) - len(hbm_args))
        + [hbm] * len(hbm_args),
        out_specs=[hbm if getattr(o, "memory_space", None) == pltpu.HBM else vmem for o in out],
        scratch_shapes=list(scratch) + ([pltpu.SemaphoreType.DMA((sems,))] if sems else []),
        cost_estimate=pl.CostEstimate(flops=flops, bytes_accessed=moved, transcendentals=trans),
        compiler_params=pltpu.CompilerParams(vmem_limit_bytes=mib * 2**20),
    )(*first, *args)


def packed(a):
    rows, half = a.shape[0], a.shape[0] // 2
    tail = a[:, 3 * LANES :]
    parts = [a[:, j * LANES : (j + 1) * LANES] for j in range(3)]
    parts.append(jnp.concatenate([tail[0:half], tail[half:]], axis=1))
    fill = -(3 * rows + half) % TILE
    if fill:
        parts.append(jnp.zeros((fill, LANES), f32))
    return jnp.concatenate(parts, axis=0)


def unpacked(a, rows):
    half = rows // 2
    last = a[3 * rows : 3 * rows + half]
    tail = jnp.concatenate([last[:, 0 : LANES // 2], last[:, LANES // 2 :]], axis=0)
    return jnp.concatenate([a[j * rows : (j + 1) * rows] for j in range(3)] + [tail], axis=1)


def pack_body(pred_ref, out_hbm, wide_ref, copies):
    wide_ref[...] = packed(pred_ref[...]).astype(bf16).reshape(wide_ref.shape)
    for c in [copies.start(wide_ref, out_hbm.at[m]) for m in range(MEMBERS)]:
        c.wait()


def tile_body(pick_ref, own_ref, got_ref, out_hbm, out_ref, copies):
    at = pl.ds(pl.multiple_of(pick_ref[1] * LANES, LANES), LANES)
    own, got = own_ref[:, at].astype(f32), got_ref[K:, at].astype(f32)
    tile = jnp.where(pick_ref[0] == 1, own, got).astype(bf16)
    out_ref[...] = jnp.broadcast_to(tile[None], out_ref.shape)
    copies.start(out_ref, out_hbm).wait()


def edges_body(src_ref, ew_ref, at_hbm, at_ref, copies):
    rows, nodes = at_ref.shape
    for r in range(0, rows, K):
        j = lax.broadcasted_iota(jnp.int32, (K, nodes), 0) + r
        acc = jnp.zeros((K, nodes), f32)
        for s in range(KNB):
            acc += jnp.where(src_ref[s : s + 1, :] == j, ew_ref[s : s + 1, :], 0.0)
        at_ref[r : r + K, :] = acc.astype(bf16)
    copies.start(at_ref, at_hbm).wait()


def norm_body(
    core_ref, own_ref, near_ref, far_ref, at_hbm, rstd_hbm, keep_hbm, normed_ref, send_hbm, at_ref, li_ref, rstd_ref, copies
):
    copies.start(at_hbm, at_ref).wait()
    core = core_ref[0]
    nodes, width = own_ref.shape
    half = width // 2
    near_at = pl.multiple_of((1 - core) * (K + nodes), K)
    far_at = pl.multiple_of(core * (K + nodes), K)
    agg = dot(at_ref[pl.ds(near_at, K), :], near_ref[0:K, :], 0, 0)
    agg += dot(at_ref[K : K + nodes, :], own_ref[...], 0, 0)
    agg += dot(at_ref[pl.ds(far_at, K), :], far_ref[...], 0, 0)
    li = own_ref[...].astype(f32) + agg
    li_ref[...] = li.astype(bf16)
    mine = pl.multiple_of(core * half, half)
    theirs = pl.multiple_of((1 - core) * half, half)
    stores = [
        copies.start(li_ref.at[:, pl.ds(theirs, half)], send_hbm.at[:, pl.ds(width, half)]),
        copies.start(li_ref.at[:, pl.ds(mine, half)], keep_hbm),
    ]
    mean = jnp.mean(li, axis=-1, keepdims=True)
    dev = li - mean
    rstd = lax.rsqrt(jnp.mean(dev * dev, axis=-1, keepdims=True) + norm_eps)
    normed_ref[...] = (dev * rstd).astype(bf16)
    stores.append(copies.start(normed_ref, send_hbm.at[:, pl.ds(0, width)]))
    rstd_ref[...] = jnp.broadcast_to(rstd, rstd_ref.shape)
    stores.append(copies.start(rstd_ref, rstd_hbm))
    for c in stores:
        c.wait()


def pred_body(all_ref, own_ref, target_ref, lw_ref, out_ref):
    members = all_ref.shape[0]
    variables = own_ref.shape[0]
    coef_pair = (1.0 - (1.0 - alpha_fair) / members) / (members * (members - 1))

    def sign(a):
        return jnp.where(a > 0.0, 1.0, jnp.where(a < 0.0, -1.0, 0.0))

    own = packed(own_ref[...])
    pair_sum = jnp.zeros(own.shape, f32)
    for k in range(members):
        pair_sum += sign(own - all_ref[k].astype(f32).reshape(own.shape))
    to_target = sign(own_ref[...] - target_ref[...])
    pair_sum = unpacked(pair_sum, variables)
    grad = lw_ref[...] * (to_target / members - coef_pair * pair_sum)
    fill = jnp.zeros((out_ref.shape[0] - variables, grad.shape[1]), f32)
    out_ref[...] = jnp.concatenate([grad, fill], axis=0).astype(bf16)


def share_body(got_ref, out_hbm, copies):
    for c in [copies.start(got_ref, out_hbm.at[m]) for m in range(out_hbm.shape[0])]:
        c.wait()


def fill_weight(wg_ref, w_ref):
    cols = w_ref.shape[1] // LANES
    for g in range(wg_ref.shape[1]):
        for c in range(2):
            for x in range(cols):
                at = (2 * g + c) * TILE
                w_ref[at : at + TILE, x * LANES : (x + 1) * LANES] = wg_ref[c * cols + x, g]


def main_body(
    core_ref, wg_ref, no_ref, keep_hbm, po_hbm, wd_hbm, got_hbm, pp_hbm, send_hbm, pre_hbm, ng_hbm,
    keep_ref, po_ref, wd_ref, got_ref, pp_ref, w_ref, lo_ref, pre_ref, parts_ref, ng_ref, copies,
):
    core = core_ref[0]
    nodes, width = no_ref.shape
    half = width // 2
    cols = half // LANES
    pairs = parts_ref.shape[1] - cols
    loads = [
        [copies.start(po_hbm, po_ref), copies.start(wd_hbm, wd_ref), copies.start(keep_hbm, keep_ref)],
        [copies.start(got_hbm, got_ref), copies.start(pp_hbm, pp_ref)],
    ]
    fill_weight(wg_ref, w_ref)
    stores = []
    for part in range(2):
        p_ref = (po_ref, pp_ref)[part]
        for c in loads[part]:
            c.wait()
        wd = wd_ref[:, pl.ds(pl.multiple_of(core * half, half), half)]
        for r in range(0, nodes, 128):
            step = min(128, nodes - r)
            n = no_ref[r : r + step, :] if part == 0 else got_ref[r : r + step, 0:width]
            li = keep_ref[r : r + step, :] if part == 0 else got_ref[r : r + step, width:]
            pre = dot(n, w_ref[...])
            og = dot(p_ref[:, r : r + step], wd, 0, 0)
            cdf = 0.5 * (1.0 + lax.erf(pre * root_half))
            pdf = jnp.exp(-0.5 * pre * pre) * inv_root_two_pi
            at = part * nodes + r
            lo_ref[at : at + step, :] = (li.astype(f32) + pre * cdf).astype(bf16)
            pre_ref[at : at + step, :] = (og * (cdf + pre * pdf)).astype(bf16)
    stores.append(copies.start(pre_ref.at[pl.ds(0, nodes)], pre_hbm))
    ng_ref[...] = dot(pre_ref[nodes:, :], w_ref[...], 1, 1).astype(bf16)
    stores.append(copies.start(ng_ref, ng_hbm))
    dec = dot(po_ref[...], lo_ref[0:nodes, :]) + dot(pp_ref[...], lo_ref[nodes:, :])
    dec = jnp.concatenate([dec, jnp.zeros((MEMBERS * TILE - dec.shape[0], half), f32)], axis=0).astype(bf16)
    for m in range(MEMBERS):
        for x in range(cols):
            parts_ref[m, pairs + x] = dec[m * TILE : (m + 1) * TILE, x * LANES : (x + 1) * LANES]
    rows = 256
    for q in range(0, width, rows):
        res = dot(no_ref[:, q : q + rows], pre_ref[0:nodes, :], 0, 0)
        res += dot(got_ref[:, q : q + rows], pre_ref[nodes:, :], 0, 0)
        res = res.astype(bf16)
        first, count = q // (2 * TILE), rows // (2 * TILE)
        for g in range(count):
            for c in range(2):
                for x in range(cols):
                    at = (2 * g + c) * TILE
                    parts_ref[c * cols + x, first + g] = res[at : at + TILE, x * LANES : (x + 1) * LANES]
        last = q + rows == width
        tiles = pl.ds(first, count + (cols if last else 0))
        stores.append(copies.start(parts_ref.at[:, tiles], send_hbm.at[:, tiles]))
    for c in stores:
        c.wait()


def scatter_body(
    core_ref, wg_ref, got_ref, rstd_hbm, po_hbm, wd_hbm, pre_hbm, own_hbm, at_hbm, mid_hbm, edge_hbm, near_ref, far_ref,
    w_ref, rstd_ref, po_ref, wd_ref, pre_ref, no_ref, at_ref, ib_ref, mid_ref, edge_ref, copies,
):
    core = core_ref[0]
    nodes, width = no_ref.shape
    first = copies.start(pre_hbm, pre_ref)
    loads = [
        copies.start(po_hbm, po_ref),
        copies.start(wd_hbm, wd_ref),
        copies.start(own_hbm.at[:, pl.ds(0, width)], no_ref),
        copies.start(rstd_hbm, rstd_ref),
        copies.start(at_hbm, at_ref),
    ]
    fill_weight(wg_ref, w_ref)
    first.wait()
    ng = dot(pre_ref[...], w_ref[...], 1, 1) + got_ref[...].astype(f32)
    for c in loads:
        c.wait()
    unit = no_ref[...].astype(f32)
    og = dot(po_ref[...], wd_ref[...], 0, 0)
    mean_g = jnp.mean(ng, axis=-1, keepdims=True)
    mean_c = jnp.mean(ng * unit, axis=-1, keepdims=True)
    ig = og + rstd_ref[:, 0:1] * (ng - mean_g - unit * mean_c)
    ib_ref[...] = ig.astype(bf16)
    near_at = pl.multiple_of((1 - core) * (K + nodes), K)
    far_at = pl.multiple_of(core * (K + nodes), K)
    near_ref[...] = dot(at_ref[pl.ds(near_at, K), :], ib_ref[...]).astype(bf16)
    far_ref[...] = dot(at_ref[pl.ds(far_at, K), :], ib_ref[...]).astype(bf16)
    total = ig + dot(at_ref[K : K + nodes, :], ib_ref[...])
    mid_ref[...] = total.astype(bf16)
    edge_ref[0:K, :] = total[0:K, :]
    edge_ref[K:, :] = total[nodes - K :, :]
    for c in [copies.start(mid_ref, mid_hbm), copies.start(edge_ref, edge_hbm)]:
        c.wait()


def join_body(core_ref, near_ref, far_ref, mid_hbm, edge_hbm, out_hbm, mid_ref, edge_ref, copies):
    core = core_ref[0]
    nodes = mid_ref.shape[0]
    loads = [copies.start(mid_hbm, mid_ref), copies.start(edge_hbm, edge_ref)]
    for c in loads:
        c.wait()
    for ref, end in ((near_ref, 1 - core), (far_ref, core)):
        edge = edge_ref[pl.ds(pl.multiple_of(end * K, K), K), :] + ref[...].astype(f32)
        mid_ref[pl.ds(pl.multiple_of(end * (nodes - K), K), K), :] = edge.astype(bf16)
    copies.start(mid_ref, out_hbm.at[0]).wait()


def total_of(got_ref):
    total = got_ref[0].astype(f32)
    for i in range(1, got_ref.shape[0]):
        total += got_ref[i].astype(f32)
    return total.astype(bf16)


def sum_body(got_ref, out_hbm, out_ref, copies):
    total = total_of(got_ref)
    parts, tiles = out_ref.shape[:2]
    dec = DEC_TILES
    weights = got_ref.shape[1] - dec
    each = weights // parts
    out_ref[:, 0:each] = total[0:weights].reshape(parts, each, TILE, LANES)
    out_ref[:, each:] = jnp.broadcast_to(total[weights:][None], (parts, dec, TILE, LANES))
    copies.start(out_ref, out_hbm).wait()


def sum_last_body(got_ref, out_hbm, out_ref, copies):
    out_ref[...] = total_of(got_ref)
    for c in [copies.start(out_ref, out_hbm.at[m]) for m in range(out_hbm.shape[0])]:
        c.wait()


def final_body(core_ref, got_ref, weight_ref, dec_ref):
    core = core_ref[0]
    half = weight_ref.shape[1] // 2
    cols = half // LANES
    variables = dec_ref.shape[0]
    for c in range(2):
        for x in range(cols):
            lane = c * half + x * LANES
            weight_ref[:, lane : lane + LANES] = got_ref[(core * cols + x) * 2 + c, 0].astype(f32)
            for m in range(MEMBERS):
                rows = min(TILE, variables - m * TILE)
                if rows > 0:
                    tile = got_ref[m * 2 + c, 1 + x].astype(f32)
                    dec_ref[m * TILE : m * TILE + rows, lane : lane + LANES] = tile[0:rows, :]


def other_pair(a):
    size = lax.axis_size(GRID)
    pairs = [(i, i + (1 if i % 2 else -1)) for i in range(1, size - 1)]
    return lax.ppermute(a, GRID, pairs)


def other_core(a):
    return lax.ppermute(a, "core", [(0, 1), (1, 0)])


def over_pairs(a):
    return lax.all_to_all(a, PAIR, 0, 0, tiled=True)


def over_mem(a):
    return lax.all_to_all(a, "mem", 0, 0, tiled=True)


def on_device(
    hidden, predictions, target, area, var_weight, interior, sources, edge_weight, w_node, w_dec
):
    pairs = lax.axis_size(PAIR)
    nodes, width = hidden.shape[1:]
    half = width // 2
    cols = half // LANES
    variables = w_dec.shape[1]
    rows = -(-variables // TILE) * TILE
    core = lax.axis_index("core")
    member = lax.axis_index("mem")
    core_arg = core.astype(jnp.int32).reshape(1)
    own = hidden[0]
    vmem = pltpu.VMEM

    row_half, col_block = member // cols, member % cols
    edge = lax.dynamic_slice(own, ((1 - core) * (nodes - K), 0), (K, width))
    near = other_core(jnp.concatenate([edge, w_node]))
    pick = jnp.stack([(core == row_half).astype(jnp.int32), (core * cols + col_block).astype(jnp.int32)])
    (tiles,) = call(
        tile_body,
        [sent((pairs, TILE, LANES), bf16)],
        (w_node, near),
        [vmem((pairs, TILE, LANES), bf16)],
        core=pick,
        sems=1,
    )

    own_pred = predictions[0].astype(f32)
    pred_tiles = -(-variables * nodes // (TILE * LANES))
    (spread_pred,) = call(
        pack_body,
        [sent((MEMBERS, pred_tiles, TILE, LANES), bf16)],
        (own_pred,),
        [vmem((pred_tiles, TILE, LANES), bf16)],
        sems=MEMBERS,
    )
    every_pred = over_mem(spread_pred)
    far = other_pair(lax.dynamic_slice(own, (core * (nodes - K), 0), (K, width)))
    (at,) = call(
        edges_body, [sent((nodes + 2 * K, nodes), bf16)], (sources, edge_weight),
        [vmem((nodes + 2 * K, nodes), bf16)], sems=1,
    )
    shards = over_pairs(after(tiles, every_pred))
    rstd, keep, normed, send = call(
        norm_body,
        [sent((nodes, LANES), f32), sent((nodes, half), bf16), staged((nodes, width), bf16),
         sent((nodes, width + half), bf16)],
        (after(own, shards), near, far),
        [vmem((nodes + 2 * K, nodes), bf16), vmem((nodes, width), bf16), vmem((nodes, LANES), f32)],
        core=core_arg,
        hbm_args=(at,),
        sems=5,
        flops=2 * nodes * (nodes + 2 * K) * width,
    )
    got = other_core(send)
    loss_weight = var_weight[:, None] * (area * interior.astype(f32))[None, :]
    (pred_grad,) = call(
        pred_body,
        [shape((rows, nodes), bf16)],
        (every_pred, own_pred, target.astype(f32), loss_weight),
    )
    pred_got = other_core(pred_grad)
    dec_t = jnp.pad(w_dec.T, ((0, rows - variables), (0, 0)))

    (spread,) = call(
        share_body,
        [sent((MEMBERS, pairs, TILE, LANES), bf16)],
        (after(shards, pred_got, far, at),),
        sems=MEMBERS,
    )
    weight = over_mem(spread)

    weight_shape = vmem((width, half), bf16)
    part_shape = (MEMBERS, pairs + cols, TILE, LANES)
    parts, pre_grad, ng_send = call(
        main_body,
        [sent(part_shape, bf16), sent((nodes, half), bf16), sent((nodes, width), bf16)],
        (weight, normed),
        [vmem((nodes, half), bf16), vmem((rows, nodes), bf16),
         vmem((rows, width), bf16), vmem((nodes, width + half), bf16), vmem((rows, nodes), bf16), weight_shape, vmem((2 * nodes, half), bf16),
         vmem((2 * nodes, half), bf16), vmem(part_shape, bf16), vmem((nodes, width), bf16)],
        core=core_arg,
        hbm_args=(keep, pred_grad, dec_t, got, pred_got),
        sems=16,
        flops=5 * 2 * nodes * width * half,
        trans=4 * nodes * half,
    )
    mem_parts = over_mem(parts)

    ng_got = other_core(ng_send)
    mid, edge, to_near, to_far = call(
        scatter_body,
        [sent((nodes, width), bf16), sent((2 * K, width), f32), shape((K, width), bf16), shape((K, width), bf16)],
        (weight, ng_got),
        [weight_shape, vmem((nodes, LANES), f32), vmem((rows, nodes), bf16), vmem((rows, width), bf16),
         vmem((nodes, half), bf16), vmem((nodes, width), bf16), vmem((nodes + 2 * K, nodes), bf16),
         vmem((nodes, width), bf16), vmem((nodes, width), bf16), vmem((2 * K, width), f32)],
        core=core_arg,
        hbm_args=(rstd, pred_grad, dec_t, pre_grad, send, at),
        sems=8,
        flops=2 * nodes * (nodes + 2 * K) * width,
    )
    from_near = other_core(to_near)
    from_far = other_pair(to_far)
    n_z, n_y = lax.axis_size("z"), lax.axis_size("y")
    (z_out,) = call(
        sum_body,
        [sent((n_z, n_y + cols, TILE, LANES), bf16)],
        (after(mem_parts, to_near),),
        [vmem((n_z, n_y + cols, TILE, LANES), bf16)],
        sems=1,
    )
    z_parts = lax.all_to_all(z_out, "z", 0, 0, tiled=True)
    (y_out,) = call(
        sum_body,
        [sent((n_y, 1 + cols, TILE, LANES), bf16)],
        (after(z_parts, from_near),),
        [vmem((n_y, 1 + cols, TILE, LANES), bf16)],
        sems=1,
    )
    y_parts = lax.all_to_all(y_out, "y", 0, 0, tiled=True)
    (hidden_grad,) = call(
        join_body,
        [sent((1, nodes, width), bf16)],
        (from_near, from_far),
        [vmem((nodes, width), bf16), vmem((2 * K, width), f32)],
        core=core_arg,
        hbm_args=(mid, edge),
        sems=3,
    )
    (last_out,) = call(
        sum_last_body,
        [sent((2 * MEMBERS, 1 + cols, TILE, LANES), bf16)],
        (after(y_parts, hidden_grad),),
        [vmem((1 + cols, TILE, LANES), bf16)],
        sems=2 * MEMBERS,
    )
    last = lax.all_to_all(last_out, ("mem", "core"), 0, 0, tiled=True)
    weight_grad, decoder_grad = call(
        final_body,
        [shape((TILE, width), f32), shape((variables, width), f32)],
        (last,),
        core=core_arg,
    )
    return (hidden_grad, weight_grad, decoder_grad.T)


def solution(mesh):
    members, blocks = mesh.shape["mem"], mesh.shape["grid"]
    split = jax.sharding.Mesh(mesh.devices.reshape(members, blocks // 8, 4, 2), ("mem",) + GRID)
    grid = GRID
    placed = (
        P("mem", grid, None),
        P("mem", None, grid),
        P(None, grid),
        P(grid),
        P(),
        P(grid),
        P(None, grid),
        P(None, grid),
        P(grid, None),
        P(),
    )
    return jax.shard_map(
        on_device,
        mesh=split,
        in_specs=placed,
        out_specs=(P("mem", grid, None), P(grid, None), P()),
        check_vma=False,
    )
```

```python
import math

import jax
import jax.numpy as jnp
from jax import lax
from jax.experimental import pallas as pl
from jax.experimental.pallas import tpu as pltpu
from jax.sharding import PartitionSpec as P

K = 64
KNB = 8
LANES = 128
TILE = 16
DEC_TILES = 4
MEMBERS = 8
GRID = ("z", "y", "core")
PAIR = ("z", "y")

norm_eps = 1e-05
alpha_fair = 0.95
root_half = 1.0 / math.sqrt(2.0)
inv_root_two_pi = 1.0 / math.sqrt(2.0 * math.pi)

f32 = jnp.float32
bf16 = jnp.bfloat16


def shape(dims, dtype):
    return jax.ShapeDtypeStruct(dims, dtype)


def dot(a, b, ca=1, cb=0):
    return lax.dot_general(a, b, (((ca,), (cb,)), ((), ())), preferred_element_type=f32)


class Copies:
    def __init__(self, sems):
        self.sems, self.used = sems, 0

    def start(self, src, dst):
        copy = pltpu.make_async_copy(src, dst, self.sems.at[self.used])
        self.used += 1
        copy.start()
        return copy


def after(x, *first):
    return lax.optimization_barrier((x,) + first)[0]


def sent(dims, dtype):
    return pltpu.HBM(dims, dtype)


def staged(dims, dtype):
    return pltpu.VMEM(dims, dtype)


def call(body, out, args, scratch=(), core=None, sems=0, hbm_args=(), flops=0, trans=0, mib=24):
    hbm_args = tuple(pltpu.with_memory_space_constraint(a, pltpu.HBM) for a in hbm_args)
    args = tuple(args) + hbm_args
    moved = sum(a.size * a.dtype.itemsize for a in args)
    moved += sum(math.prod(o.shape) * jnp.dtype(o.dtype).itemsize for o in out)
    first = [] if core is None else [core]

    def kernel(*refs):
        if sems:
            body(*refs[:-1], Copies(refs[-1]))
        else:
            body(*refs)

    vmem = pl.BlockSpec(memory_space=pltpu.VMEM)
    hbm = pl.BlockSpec(memory_space=pltpu.HBM)
    return pl.pallas_call(
        kernel,
        out_shape=out,
        in_specs=[pl.BlockSpec(memory_space=pltpu.SMEM)] * len(first) + [vmem] * (len(args) - len(hbm_args))
        + [hbm] * len(hbm_args),
        out_specs=[hbm if getattr(o, "memory_space", None) == pltpu.HBM else vmem for o in out],
        scratch_shapes=list(scratch) + ([pltpu.SemaphoreType.DMA((sems,))] if sems else []),
        cost_estimate=pl.CostEstimate(flops=flops, bytes_accessed=moved, transcendentals=trans),
        compiler_params=pltpu.CompilerParams(vmem_limit_bytes=mib * 2**20),
    )(*first, *args)


def packed(a):
    rows, half = a.shape[0], a.shape[0] // 2
    tail = a[:, 3 * LANES :]
    parts = [a[:, j * LANES : (j + 1) * LANES] for j in range(3)]
    parts.append(jnp.concatenate([tail[0:half], tail[half:]], axis=1))
    fill = -(3 * rows + half) % TILE
    if fill:
        parts.append(jnp.zeros((fill, LANES), f32))
    return jnp.concatenate(parts, axis=0)


def unpacked(a, rows):
    half = rows // 2
    last = a[3 * rows : 3 * rows + half]
    tail = jnp.concatenate([last[:, 0 : LANES // 2], last[:, LANES // 2 :]], axis=0)
    return jnp.concatenate([a[j * rows : (j + 1) * rows] for j in range(3)] + [tail], axis=1)


def pack_body(pred_ref, out_hbm, wide_ref, copies):
    wide_ref[...] = packed(pred_ref[...]).astype(bf16).reshape(wide_ref.shape)
    for c in [copies.start(wide_ref, out_hbm.at[m]) for m in range(MEMBERS)]:
        c.wait()


def tile_body(pick_ref, own_ref, got_ref, out_hbm, out_ref, copies):
    at = pl.ds(pl.multiple_of(pick_ref[1] * LANES, LANES), LANES)
    own, got = own_ref[:, at].astype(f32), got_ref[K:, at].astype(f32)
    tile = jnp.where(pick_ref[0] == 1, own, got).astype(bf16)
    out_ref[...] = jnp.broadcast_to(tile[None], out_ref.shape)
    copies.start(out_ref, out_hbm).wait()


def edges_body(src_ref, ew_ref, at_hbm, at_ref, copies):
    rows, nodes = at_ref.shape
    for r in range(0, rows, K):
        j = lax.broadcasted_iota(jnp.int32, (K, nodes), 0) + r
        acc = jnp.zeros((K, nodes), f32)
        for s in range(KNB):
            acc += jnp.where(src_ref[s : s + 1, :] == j, ew_ref[s : s + 1, :], 0.0)
        at_ref[r : r + K, :] = acc.astype(bf16)
    copies.start(at_ref, at_hbm).wait()


def norm_body(
    core_ref, own_ref, near_ref, far_ref, at_hbm, rstd_hbm, keep_hbm, normed_ref, send_hbm, at_ref, li_ref, rstd_ref, copies
):
    copies.start(at_hbm, at_ref).wait()
    core = core_ref[0]
    nodes, width = own_ref.shape
    half = width // 2
    near_at = pl.multiple_of((1 - core) * (K + nodes), K)
    far_at = pl.multiple_of(core * (K + nodes), K)
    agg = dot(at_ref[pl.ds(near_at, K), :], near_ref[0:K, :], 0, 0)
    agg += dot(at_ref[K : K + nodes, :], own_ref[...], 0, 0)
    agg += dot(at_ref[pl.ds(far_at, K), :], far_ref[...], 0, 0)
    li = own_ref[...].astype(f32) + agg
    li_ref[...] = li.astype(bf16)
    mine = pl.multiple_of(core * half, half)
    theirs = pl.multiple_of((1 - core) * half, half)
    stores = [
        copies.start(li_ref.at[:, pl.ds(theirs, half)], send_hbm.at[:, pl.ds(width, half)]),
        copies.start(li_ref.at[:, pl.ds(mine, half)], keep_hbm),
    ]
    mean = jnp.mean(li, axis=-1, keepdims=True)
    dev = li - mean
    rstd = lax.rsqrt(jnp.mean(dev * dev, axis=-1, keepdims=True) + norm_eps)
    normed_ref[...] = (dev * rstd).astype(bf16)
    stores.append(copies.start(normed_ref, send_hbm.at[:, pl.ds(0, width)]))
    rstd_ref[...] = jnp.broadcast_to(rstd, rstd_ref.shape)
    stores.append(copies.start(rstd_ref, rstd_hbm))
    for c in stores:
        c.wait()


def pred_body(all_ref, own_ref, target_ref, lw_ref, out_ref):
    members = all_ref.shape[0]
    variables = own_ref.shape[0]
    coef_pair = (1.0 - (1.0 - alpha_fair) / members) / (members * (members - 1))

    def sign(a):
        return jnp.where(a > 0.0, 1.0, jnp.where(a < 0.0, -1.0, 0.0))

    own = packed(own_ref[...])
    pair_sum = jnp.zeros(own.shape, f32)
    for k in range(members):
        pair_sum += sign(own - all_ref[k].astype(f32).reshape(own.shape))
    to_target = sign(own_ref[...] - target_ref[...])
    pair_sum = unpacked(pair_sum, variables)
    grad = lw_ref[...] * (to_target / members - coef_pair * pair_sum)
    fill = jnp.zeros((out_ref.shape[0] - variables, grad.shape[1]), f32)
    out_ref[...] = jnp.concatenate([grad, fill], axis=0).astype(bf16)


def share_body(got_ref, out_hbm, copies):
    for c in [copies.start(got_ref, out_hbm.at[m]) for m in range(out_hbm.shape[0])]:
        c.wait()


def fill_weight(wg_ref, w_ref):
    cols = w_ref.shape[1] // LANES
    for g in range(wg_ref.shape[1]):
        for c in range(2):
            for x in range(cols):
                at = (2 * g + c) * TILE
                w_ref[at : at + TILE, x * LANES : (x + 1) * LANES] = wg_ref[c * cols + x, g]


def main_body(
    core_ref, wg_ref, no_ref, keep_hbm, po_hbm, wd_hbm, got_hbm, pp_hbm, send_hbm, pre_hbm, ng_hbm,
    keep_ref, po_ref, wd_ref, got_ref, pp_ref, w_ref, lo_ref, pre_ref, parts_ref, ng_ref, copies,
):
    core = core_ref[0]
    nodes, width = no_ref.shape
    half = width // 2
    cols = half // LANES
    pairs = parts_ref.shape[1] - cols
    loads = [
        [copies.start(po_hbm, po_ref), copies.start(wd_hbm, wd_ref), copies.start(keep_hbm, keep_ref)],
        [copies.start(got_hbm, got_ref), copies.start(pp_hbm, pp_ref)],
    ]
    fill_weight(wg_ref, w_ref)
    stores = []
    for part in range(2):
        p_ref = (po_ref, pp_ref)[part]
        for c in loads[part]:
            c.wait()
        wd = wd_ref[:, pl.ds(pl.multiple_of(core * half, half), half)]
        for r in range(0, nodes, 128):
            step = min(128, nodes - r)
            n = no_ref[r : r + step, :] if part == 0 else got_ref[r : r + step, 0:width]
            li = keep_ref[r : r + step, :] if part == 0 else got_ref[r : r + step, width:]
            pre = dot(n, w_ref[...])
            og = dot(p_ref[:, r : r + step], wd, 0, 0)
            cdf = 0.5 * (1.0 + lax.erf(pre * root_half))
            pdf = jnp.exp(-0.5 * pre * pre) * inv_root_two_pi
            at = part * nodes + r
            lo_ref[at : at + step, :] = (li.astype(f32) + pre * cdf).astype(bf16)
            pre_ref[at : at + step, :] = (og * (cdf + pre * pdf)).astype(bf16)
    stores.append(copies.start(pre_ref.at[pl.ds(0, nodes)], pre_hbm))
    ng_ref[...] = dot(pre_ref[nodes:, :], w_ref[...], 1, 1).astype(bf16)
    stores.append(copies.start(ng_ref, ng_hbm))
    dec = dot(po_ref[...], lo_ref[0:nodes, :]) + dot(pp_ref[...], lo_ref[nodes:, :])
    dec = jnp.concatenate([dec, jnp.zeros((MEMBERS * TILE - dec.shape[0], half), f32)], axis=0).astype(bf16)
    for m in range(MEMBERS):
        for x in range(cols):
            parts_ref[m, pairs + x] = dec[m * TILE : (m + 1) * TILE, x * LANES : (x + 1) * LANES]
    rows = 256
    for q in range(0, width, rows):
        res = dot(no_ref[:, q : q + rows], pre_ref[0:nodes, :], 0, 0)
        res += dot(got_ref[:, q : q + rows], pre_ref[nodes:, :], 0, 0)
        res = res.astype(bf16)
        first, count = q // (2 * TILE), rows // (2 * TILE)
        for g in range(count):
            for c in range(2):
                for x in range(cols):
                    at = (2 * g + c) * TILE
                    parts_ref[c * cols + x, first + g] = res[at : at + TILE, x * LANES : (x + 1) * LANES]
        last = q + rows == width
        tiles = pl.ds(first, count + (cols if last else 0))
        stores.append(copies.start(parts_ref.at[:, tiles], send_hbm.at[:, tiles]))
    for c in stores:
        c.wait()


def scatter_body(
    core_ref, wg_ref, got_ref, rstd_hbm, po_hbm, wd_hbm, pre_hbm, own_hbm, at_hbm, mid_hbm, edge_hbm, near_ref, far_ref,
    w_ref, rstd_ref, po_ref, wd_ref, pre_ref, no_ref, at_ref, ib_ref, mid_ref, edge_ref, copies,
):
    core = core_ref[0]
    nodes, width = no_ref.shape
    first = copies.start(pre_hbm, pre_ref)
    loads = [
        copies.start(po_hbm, po_ref),
        copies.start(wd_hbm, wd_ref),
        copies.start(own_hbm.at[:, pl.ds(0, width)], no_ref),
        copies.start(rstd_hbm, rstd_ref),
        copies.start(at_hbm, at_ref),
    ]
    fill_weight(wg_ref, w_ref)
    first.wait()
    ng = dot(pre_ref[...], w_ref[...], 1, 1) + got_ref[...].astype(f32)
    for c in loads:
        c.wait()
    unit = no_ref[...].astype(f32)
    og = dot(po_ref[...], wd_ref[...], 0, 0)
    mean_g = jnp.mean(ng, axis=-1, keepdims=True)
    mean_c = jnp.mean(ng * unit, axis=-1, keepdims=True)
    ig = og + rstd_ref[:, 0:1] * (ng - mean_g - unit * mean_c)
    ib_ref[...] = ig.astype(bf16)
    near_at = pl.multiple_of((1 - core) * (K + nodes), K)
    far_at = pl.multiple_of(core * (K + nodes), K)
    near_ref[...] = dot(at_ref[pl.ds(near_at, K), :], ib_ref[...]).astype(bf16)
    far_ref[...] = dot(at_ref[pl.ds(far_at, K), :], ib_ref[...]).astype(bf16)
    total = ig + dot(at_ref[K : K + nodes, :], ib_ref[...])
    mid_ref[...] = total.astype(bf16)
    edge_ref[0:K, :] = total[0:K, :]
    edge_ref[K:, :] = total[nodes - K :, :]
    for c in [copies.start(mid_ref, mid_hbm), copies.start(edge_ref, edge_hbm)]:
        c.wait()


def join_body(core_ref, near_ref, far_ref, mid_hbm, edge_hbm, out_hbm, mid_ref, edge_ref, copies):
    core = core_ref[0]
    nodes = mid_ref.shape[0]
    loads = [copies.start(mid_hbm, mid_ref), copies.start(edge_hbm, edge_ref)]
    for c in loads:
        c.wait()
    for ref, end in ((near_ref, 1 - core), (far_ref, core)):
        edge = edge_ref[pl.ds(pl.multiple_of(end * K, K), K), :] + ref[...].astype(f32)
        mid_ref[pl.ds(pl.multiple_of(end * (nodes - K), K), K), :] = edge.astype(bf16)
    copies.start(mid_ref, out_hbm.at[0]).wait()


def total_of(got_ref):
    total = got_ref[0].astype(f32)
    for i in range(1, got_ref.shape[0]):
        total += got_ref[i].astype(f32)
    return total.astype(bf16)


def sum_body(got_ref, out_hbm, out_ref, copies):
    total = total_of(got_ref)
    parts, tiles = out_ref.shape[:2]
    dec = DEC_TILES
    weights = got_ref.shape[1] - dec
    each = weights // parts
    out_ref[:, 0:each] = total[0:weights].reshape(parts, each, TILE, LANES)
    out_ref[:, each:] = jnp.broadcast_to(total[weights:][None], (parts, dec, TILE, LANES))
    copies.start(out_ref, out_hbm).wait()


def sum_last_body(got_ref, out_hbm, out_ref, copies):
    out_ref[...] = total_of(got_ref)
    for c in [copies.start(out_ref, out_hbm.at[m]) for m in range(out_hbm.shape[0])]:
        c.wait()


def final_body(core_ref, got_ref, weight_ref, dec_ref):
    core = core_ref[0]
    half = weight_ref.shape[1] // 2
    cols = half // LANES
    variables = dec_ref.shape[0]
    for c in range(2):
        for x in range(cols):
            lane = c * half + x * LANES
            weight_ref[:, lane : lane + LANES] = got_ref[(core * cols + x) * 2 + c, 0].astype(f32)
            for m in range(MEMBERS):
                rows = min(TILE, variables - m * TILE)
                if rows > 0:
                    tile = got_ref[m * 2 + c, 1 + x].astype(f32)
                    dec_ref[m * TILE : m * TILE + rows, lane : lane + LANES] = tile[0:rows, :]


def other_pair(a):
    size = lax.axis_size(GRID)
    pairs = [(i, i + (1 if i % 2 else -1)) for i in range(1, size - 1)]
    return lax.ppermute(a, GRID, pairs)


def other_core(a):
    return lax.ppermute(a, "core", [(0, 1), (1, 0)])


def over_pairs(a):
    return lax.all_to_all(a, PAIR, 0, 0, tiled=True)


def over_mem(a):
    return lax.all_to_all(a, "mem", 0, 0, tiled=True)


def on_device(
    hidden, predictions, target, area, var_weight, interior, sources, edge_weight, w_node, w_dec
):
    pairs = lax.axis_size(PAIR)
    nodes, width = hidden.shape[1:]
    half = width // 2
    cols = half // LANES
    variables = w_dec.shape[1]
    rows = -(-variables // TILE) * TILE
    core = lax.axis_index("core")
    member = lax.axis_index("mem")
    core_arg = core.astype(jnp.int32).reshape(1)
    own = hidden[0]
    vmem = pltpu.VMEM

    row_half, col_block = member // cols, member % cols
    edge = lax.dynamic_slice(own, ((1 - core) * (nodes - K), 0), (K, width))
    near = other_core(jnp.concatenate([edge, w_node]))
    pick = jnp.stack([(core == row_half).astype(jnp.int32), (core * cols + col_block).astype(jnp.int32)])
    (tiles,) = call(
        tile_body,
        [sent((pairs, TILE, LANES), bf16)],
        (w_node, near),
        [vmem((pairs, TILE, LANES), bf16)],
        core=pick,
        sems=1,
    )

    own_pred = predictions[0].astype(f32)
    pred_tiles = -(-variables * nodes // (TILE * LANES))
    (spread_pred,) = call(
        pack_body,
        [sent((MEMBERS, pred_tiles, TILE, LANES), bf16)],
        (own_pred,),
        [vmem((pred_tiles, TILE, LANES), bf16)],
        sems=MEMBERS,
    )
    every_pred = over_mem(spread_pred)
    far = other_pair(lax.dynamic_slice(own, (core * (nodes - K), 0), (K, width)))
    (at,) = call(
        edges_body, [sent((nodes + 2 * K, nodes), bf16)], (sources, edge_weight),
        [vmem((nodes + 2 * K, nodes), bf16)], sems=1,
    )
    shards = over_pairs(after(tiles, every_pred))
    rstd, keep, normed, send = call(
        norm_body,
        [sent((nodes, LANES), f32), sent((nodes, half), bf16), staged((nodes, width), bf16),
         sent((nodes, width + half), bf16)],
        (after(own, shards), near, far),
        [vmem((nodes + 2 * K, nodes), bf16), vmem((nodes, width), bf16), vmem((nodes, LANES), f32)],
        core=core_arg,
        hbm_args=(at,),
        sems=5,
        flops=2 * nodes * (nodes + 2 * K) * width,
    )
    got = other_core(send)
    loss_weight = var_weight[:, None] * (area * interior.astype(f32))[None, :]
    (pred_grad,) = call(
        pred_body,
        [shape((rows, nodes), bf16)],
        (every_pred, own_pred, target.astype(f32), loss_weight),
    )
    pred_got = other_core(pred_grad)
    dec_t = jnp.pad(w_dec.T, ((0, rows - variables), (0, 0)))

    (spread,) = call(
        share_body,
        [sent((MEMBERS, pairs, TILE, LANES), bf16)],
        (after(shards, pred_got, far, at),),
        sems=MEMBERS,
    )
    weight = over_mem(spread)

    weight_shape = vmem((width, half), bf16)
    part_shape = (MEMBERS, pairs + cols, TILE, LANES)
    parts, pre_grad, ng_send = call(
        main_body,
        [sent(part_shape, bf16), sent((nodes, half), bf16), sent((nodes, width), bf16)],
        (weight, normed),
        [vmem((nodes, half), bf16), vmem((rows, nodes), bf16),
         vmem((rows, width), bf16), vmem((nodes, width + half), bf16), vmem((rows, nodes), bf16), weight_shape, vmem((2 * nodes, half), bf16),
         vmem((2 * nodes, half), bf16), vmem(part_shape, bf16), vmem((nodes, width), bf16)],
        core=core_arg,
        hbm_args=(keep, pred_grad, dec_t, got, pred_got),
        sems=16,
        flops=5 * 2 * nodes * width * half,
        trans=4 * nodes * half,
    )
    mem_parts = over_mem(parts)

    ng_got = other_core(ng_send)
    mid, edge, to_near, to_far = call(
        scatter_body,
        [sent((nodes, width), bf16), sent((2 * K, width), f32), shape((K, width), bf16), shape((K, width), bf16)],
        (weight, ng_got),
        [weight_shape, vmem((nodes, LANES), f32), vmem((rows, nodes), bf16), vmem((rows, width), bf16),
         vmem((nodes, half), bf16), vmem((nodes, width), bf16), vmem((nodes + 2 * K, nodes), bf16),
         vmem((nodes, width), bf16), vmem((nodes, width), bf16), vmem((2 * K, width), f32)],
        core=core_arg,
        hbm_args=(rstd, pred_grad, dec_t, pre_grad, send, at),
        sems=8,
        flops=2 * nodes * (nodes + 2 * K) * width,
    )
    from_near = other_core(to_near)
    from_far = other_pair(to_far)
    n_z, n_y = lax.axis_size("z"), lax.axis_size("y")
    (z_out,) = call(
        sum_body,
        [sent((n_z, n_y + cols, TILE, LANES), bf16)],
        (after(mem_parts, from_near),),
        [vmem((n_z, n_y + cols, TILE, LANES), bf16)],
        sems=1,
    )
    z_parts = lax.all_to_all(z_out, "z", 0, 0, tiled=True)
    (y_out,) = call(
        sum_body,
        [sent((n_y, 1 + cols, TILE, LANES), bf16)],
        (after(z_parts, to_far),),
        [vmem((n_y, 1 + cols, TILE, LANES), bf16)],
        sems=1,
    )
    y_parts = lax.all_to_all(y_out, "y", 0, 0, tiled=True)
    (hidden_grad,) = call(
        join_body,
        [sent((1, nodes, width), bf16)],
        (from_near, from_far),
        [vmem((nodes, width), bf16), vmem((2 * K, width), f32)],
        core=core_arg,
        hbm_args=(mid, edge),
        sems=3,
    )
    (last_out,) = call(
        sum_last_body,
        [sent((2 * MEMBERS, 1 + cols, TILE, LANES), bf16)],
        (after(y_parts, hidden_grad),),
        [vmem((1 + cols, TILE, LANES), bf16)],
        sems=2 * MEMBERS,
    )
    last = lax.all_to_all(last_out, ("mem", "core"), 0, 0, tiled=True)
    weight_grad, decoder_grad = call(
        final_body,
        [shape((TILE, width), f32), shape((variables, width), f32)],
        (last,),
        core=core_arg,
    )
    return (hidden_grad, weight_grad, decoder_grad.T)


def solution(mesh):
    members, blocks = mesh.shape["mem"], mesh.shape["grid"]
    split = jax.sharding.Mesh(mesh.devices.reshape(members, blocks // 8, 4, 2), ("mem",) + GRID)
    grid = GRID
    placed = (
        P("mem", grid, None),
        P("mem", None, grid),
        P(None, grid),
        P(grid),
        P(),
        P(grid),
        P(None, grid),
        P(None, grid),
        P(grid, None),
        P(),
    )
    return jax.shard_map(
        on_device,
        mesh=split,
        in_specs=placed,
        out_specs=(P("mem", grid, None), P(grid, None), P()),
        check_vma=False,
    )
```
